256 devices in a mesh: gz: 4 (over y), row: 8 (over z), col: 8 (over x, core).
Axes of the slice: x: 4, y: 4, z: 8, core: 2. Of those that a mesh axis runs over, the one named last changes fastest.
Arguments:
- diag_parts: float32 [4, 512, 512], P('gz', 'row', 'col'), as said below
- column_parts: float32 [4, 8192, 512], P('gz', 'row', 'col'), may hold values from -6 to 6
- row_parts: float32 [4, 512, 8192], P('gz', 'row', 'col'), may hold values from -2.1 to 2.1
- schur_parts: float32 [4, 8192, 8192], P('gz', 'row', 'col'), may hold values from -6 to 6
- block_pattern: int32 [4, 64, 64], P('gz', 'row', 'col'), may hold values 0 or 1
- pivot_order: int32 [512], replicated, may hold values from 0 to 511, as said below
Outputs:
- factor_diag: float32 [512, 512], P('row', 'col')
- lower_panel: float32 [8192, 512], P('row', 'col')
- upper_panel: float32 [512, 8192], P('row', 'col')
- schur_out: float32 [8192, 8192], P('row', 'col')
The draws below stay inside these ranges and needn't reach their ends.
Inputs may be any that keep to these rules, and one draw needn't show every extreme that they name: `pivot_order`: a permutation of 0 to 511. For every layer g the rows of diag_parts[g] taken in the order pivot_order form a symmetric matrix; the sum over layers so reordered is symmetric positive definite with smallest eigenvalue at least 8.
All inputs are finite; a program needn't handle non-finite values. No bound on the sum of `block_pattern` on one device may be relied on, other than what follows from the above.
Results may differ from the reference program's by a relative error of at most 0.00013.
Values sent between devices are 32-bit elements; how exact they have to be, the bound alone decides.
A program may use at most 64 MiB of HBM per device.

```python
import jax
import jax.numpy as jnp
from jax import lax

W = 512
BS = 128
LAYERS = 4
ROWS = 8192
COLS = 8192


def pivot_rows(key):
    return jax.random.permutation(jax.random.fold_in(key, 17), W).astype(jnp.int32)


def draw_pivot_order(key, part):
    return pivot_rows(key)


def gram_matrix(base):
    product = jnp.dot(base, base.T, precision=lax.Precision.HIGHEST, preferred_element_type=jnp.float32)
    return 0.5 * (product + product.T) / W


def draw_diag_parts(key, part):
    order = pivot_rows(key)
    key = jax.random.fold_in(key, 3)
    gram_key, other_key, shift_key = jax.random.split(key, 3)
    base = jax.random.normal(gram_key, (W, W), jnp.float32)
    identity = jnp.eye(W, dtype=jnp.float32)
    shift = jax.random.uniform(shift_key, (W,), jnp.float32, 0.5, 1.0)
    leading = 16.0 * (gram_matrix(base) + identity * shift[None, :])
    others = jax.random.normal(other_key, (LAYERS, W, W), jnp.float32)
    other_grams = jax.vmap(gram_matrix)(others)
    layer = jnp.arange(LAYERS)
    other_weight = jnp.where(layer == 0, 0.0, 4.0 / max(LAYERS - 1, 1)).astype(jnp.float32)
    owner = jnp.where(layer == 0, 1.0, 0.0).astype(jnp.float32)
    symmetric = other_grams * other_weight[:, None, None] + owner[:, None, None] * leading[None, :, :]
    return jnp.zeros((LAYERS, W, W), jnp.float32).at[:, order, :].set(symmetric)


def with_ends(values, rng, least, high):
    longest = values.shape.index(max(values.shape))
    spots = []
    for shift in (0, 1):
        where = [jax.random.randint(jax.random.fold_in(rng, axis), (), 0, length) for axis, length in enumerate(values.shape)]
        where[longest] = (where[longest] + shift) % values.shape[longest]
        spots.append(tuple(where))
    return values.at[spots[0]].set(least).at[spots[1]].set(high)


def shard_levels(stream_key, dims, shards, smallest, largest):
    level, own = 1.0, jax.random.fold_in(stream_key, 6)
    for position, blocks in shards:
        heights = jnp.exp(jax.random.uniform(jax.random.fold_in(own, position), (blocks,), jnp.float32, smallest / len(shards), largest / len(shards)))
        level = level * jnp.repeat(heights, dims[position] // blocks).reshape([-1 if axis == position else 1 for axis in range(len(dims))])
    return level


def normal_values(key, extent, scale, bound, shards=(), held_as=jnp.bfloat16):
    values = scale * jax.random.normal(key, extent, jnp.float32)
    if shards:
        values = values * shard_levels(key, extent, shards, -0.22, 0.18)
    return jnp.clip(values, -bound, bound).astype(held_as)


def setup_inputs(seed: int = 0) -> dict:
    key_of = jax.random.split(jax.random.key(seed), 7)
    diag_parts = draw_diag_parts(jax.random.fold_in(key_of[6], 71), 0)
    column_parts = normal_values(key_of[1], (LAYERS, ROWS, W), 1.0, 6.0, ((0, 4), (1, 8), (2, 8)), jnp.float32)
    row_parts = normal_values(key_of[2], (LAYERS, W, COLS), 0.35, 2.1, ((0, 4), (1, 8), (2, 8)), jnp.float32)
    schur_parts = normal_values(key_of[3], (LAYERS, ROWS, COLS), 1.0, 6.0, ((0, 4), (1, 8), (2, 8)), jnp.float32)
    block_pattern = with_ends((jax.random.randint(key_of[4], (LAYERS, ROWS // BS, COLS // BS), 0, 3) < 2).astype(jnp.int32), jax.random.fold_in(key_of[4], 1), 0, 1)
    pivot_order = draw_pivot_order(jax.random.fold_in(key_of[6], 71), 0)
    return {"diag_parts": diag_parts, "column_parts": column_parts, "row_parts": row_parts, "schur_parts": schur_parts, "block_pattern": block_pattern, "pivot_order": pivot_order}


def reference(diag_parts, column_parts, row_parts, schur_parts, block_pattern, pivot_order):
    diag_sum = jnp.sum(diag_parts, axis=0)
    column_sum = jnp.sum(column_parts, axis=0)
    row_sum = jnp.sum(row_parts, axis=0)
    total_rows = schur_parts.shape[1]
    total_cols = schur_parts.shape[2]
    schur_sum = jnp.zeros((total_rows, total_cols), jnp.float32)
    for layer in range(LAYERS):
        blocks = schur_parts[layer].reshape(total_rows // BS, BS, total_cols // BS, BS)
        weights = block_pattern[layer].astype(jnp.float32)[:, None, :, None]
        schur_sum = schur_sum + (blocks * weights).reshape(total_rows, total_cols)
    pivoted = jnp.take(diag_sum, pivot_order, axis=0)
    factor_diag = jnp.linalg.cholesky(pivoted)
    lower_panel = jax.scipy.linalg.solve_triangular(factor_diag, column_sum.T, lower=True).T
    upper_panel = jax.scipy.linalg.solve_triangular(factor_diag, jnp.take(row_sum, pivot_order, axis=0), lower=True)
    schur_out = schur_sum - jnp.dot(lower_panel.astype(jnp.float32), upper_panel.astype(jnp.float32), precision=lax.Precision.HIGHEST, preferred_element_type=jnp.float32)
    return (factor_diag, lower_panel, upper_panel, schur_out)
```

```python
import functools

import jax
import jax.numpy as jnp
from jax import lax
from jax.experimental import pallas as pl
from jax.experimental.pallas import tpu as pltpu
from jax.sharding import PartitionSpec as P

BS = 128
LAYERS = 4
PANEL = 16
HALF = PANEL + BS
SUBS = ((0, 16), (16, 32), (48, 32), (80, 32), (112, 32))
HI = lax.Precision.HIGHEST
F32 = jnp.float32
BF16 = jnp.bfloat16
MESH = pl.DeviceIdType.MESH


def split2(x):
    hi = x.astype(BF16)
    return hi, (x - hi.astype(F32)).astype(BF16)


def split3(x):
    hi = x.astype(BF16)
    rest = x - hi.astype(F32)
    mid = rest.astype(BF16)
    return hi, mid, (rest - mid.astype(F32)).astype(BF16)


def contract(a, b, da, db):
    return lax.dot_general(a, b, (((da,), (db,)), ((), ())), preferred_element_type=F32)


def dot3(a, b):
    return contract(a[0], b[0], 1, 0) + (contract(a[0], b[1], 1, 0) + contract(a[1], b[0], 1, 0))


def eliminate_group(d_ref, q):
    lane = lax.broadcasted_iota(jnp.int32, (8, 128), 1)
    sub = lax.broadcasted_iota(jnp.int32, (8, 128), 0)
    lo = 8 * q
    g = d_ref[lo : lo + 8, :]
    col = [jnp.broadcast_to(g[:, lo + j : lo + j + 1], (8, 128)) for j in range(8)]
    snap = jnp.zeros((8, 128), F32)
    pivots = jnp.ones((8, 128), F32)
    for k in range(8):
        piv = jnp.broadcast_to(col[k][k : k + 1, :], (8, 128))
        f = jnp.where(sub != k, col[k] * (1.0 / piv), 0.0)
        for j in range(k + 1, 8):
            col[j] = col[j] - f * jnp.broadcast_to(col[j][k : k + 1, :], (8, 128))
        g = jnp.where(lane == lo + k, jnp.where(sub == k, 1.0, 0.0), g)
        top = jnp.broadcast_to(g[k : k + 1, :], (8, 128))
        snap = jnp.where(sub == k, top, snap)
        pivots = jnp.where(sub == k, piv, pivots)
        g = g - f * top
    w = g / pivots
    if q < 15:
        n = 120 - lo
        below = d_ref[lo + 8 : 128, :]
        lane_b = lax.broadcasted_iota(jnp.int32, (n, 128), 1)
        acc = jnp.where((lane_b >= lo) & (lane_b < lo + 8), 0.0, below)
        for j in range(8):
            acc = acc - jnp.broadcast_to(below[:, lo + j : lo + j + 1], (n, 128)) * jnp.broadcast_to(
                w[j : j + 1, :], (n, 128)
            )
        d_ref[lo + 8 : 128, :] = acc
    d_ref[lo : lo + 8, :] = jnp.where(lane == lo + sub, 1.0, snap) * lax.rsqrt(pivots)
    return jnp.sqrt(pivots)


def eliminate_block(a_ref, d_ref, i, hook):
    width = a_ref.shape[0]
    at = pl.multiple_of(i * 128, 128)
    rows = pl.ds(at, 128)
    d_ref[...] = a_ref[rows, pl.ds(at, 128)]
    diagonal = []
    for q in range(16):
        if q % 4 == 0:
            hook(i, q // 4)
        diagonal.append(eliminate_group(d_ref, q))
    r = lax.broadcasted_iota(jnp.int32, (128, 128), 0)
    c = lax.broadcasted_iota(jnp.int32, (128, 128), 1)
    d = d_ref[...]
    inverse = jnp.where(c <= r, d, 0.0)
    upper = jnp.where(c > r, d, jnp.where(c == r, jnp.concatenate(diagonal, axis=0), 0.0))
    p = jnp.dot(inverse, a_ref[rows, :], precision=HI, preferred_element_type=F32)
    left = lax.broadcasted_iota(jnp.int32, (128, width), 1)
    right_of = jnp.where(left >= at + 128, p[:, :width], 0.0)
    a_ref[...] = a_ref[...] - lax.dot_general(
        right_of, p, (((0,), (0,)), ((), ())), precision=HI, preferred_element_type=F32
    )
    a_ref[rows, :] = jnp.concatenate([right_of, p[:, width:]], axis=1)
    a_ref[rows, pl.ds(at, 128)] = upper


def kernel(
    grid_rows, grid_cols,
    diag_ref, pattern_ref, pivot_ref, column_ref, row_ref, schur_ref,
    factor_out, lower_out, upper_out, schur_out,
    w, fin, rs1, rsx, column_v, row_v, factor_v, weights,
    layer_diag, grid_diag, full_diag, all_columns, all_rows, a_ref, d_ref, left_x, right_x, update,
    load_sem, y_send, y_recv, dy_send, dy_recv, dz_send, dz_recv, dx_send, dx_recv,
    pz_send, pz_recv, px_send, px_recv, out_sem,
):
    m = lax.axis_index("gz")
    r = lax.axis_index("row")
    c = lax.axis_index("col")
    width = a_ref.shape[0]
    span = fin.shape[3]
    blocks = width // 128

    def layer(k):
        return lax.rem(m + k + LAYERS, LAYERS)

    def row_peer(k):
        return lax.rem(r + k, grid_rows)

    def col_peer(k):
        return lax.rem(c + k, grid_cols)

    load_column = pltpu.make_async_copy(column_ref, column_v, load_sem.at[8])
    load_row = pltpu.make_async_copy(row_ref, row_v, load_sem.at[9])
    load_column.start()
    load_row.start()

    def load_front(k, h):
        block = k * 2 + h
        return pltpu.make_async_copy(
            schur_ref.at[pl.ds(pl.multiple_of(block * BS, BS), BS), :],
            w.at[k, h, pl.ds(PANEL, BS), :],
            load_sem.at[block],
        )

    order = [(layer(k), h) for k in (2, 1, -1, 0) for h in range(2)]
    for k, h in order:
        load_front(k, h).start()

    barrier = pltpu.get_barrier_semaphore()
    for k in range(1, LAYERS):
        pl.semaphore_signal(barrier, inc=1, device_id=(layer(k), r, c), device_id_type=MESH)
    for k in range(1, grid_rows):
        pl.semaphore_signal(barrier, inc=1, device_id=(m, row_peer(k), c), device_id_type=MESH)
    for k in range(1, grid_cols):
        pl.semaphore_signal(barrier, inc=1, device_id=(m, r, col_peer(k)), device_id_type=MESH)
    pl.semaphore_wait(barrier, LAYERS - 1 + grid_rows - 1 + grid_cols - 1)

    def ring(t, d, s):
        step = 1 - 2 * d
        to = layer(step)
        first, count = SUBS[s]
        rows = pl.ds(first, count)
        if t == 1:
            src, dst = w.at[layer(2), d, rows], rs1.at[d, rows]
        elif t == 2:
            src, dst = w.at[to, 1 - d, rows], rsx.at[d, 1 - d, rows]
        elif t == 3:
            src, dst = w.at[to, d, rows], rsx.at[d, d, rows]
        elif t == 4:
            src = dst = fin.at[m, d, rows]
        elif t == 5:
            src = dst = fin.at[m, 1 - d, rows]
        else:
            src = dst = fin.at[layer(-step), d, rows]
        return pltpu.make_async_remote_copy(
            src_ref=src, dst_ref=dst, send_sem=y_send.at[t - 1, d, s], recv_sem=y_recv.at[t - 1, d, s],
            device_id=(to, r, c), device_id_type=MESH,
        )

    def add_opposite(s):
        first, count = SUBS[s]
        rows = pl.ds(first, count)
        for d in range(2):
            ring(1, d, s).wait_recv()
            to = layer(1 - 2 * d)
            w[to, d, rows, :] = w[to, d, rows, :] + rs1[d, rows, :]
            ring(3, d, s).start()

    def finish_sum(s):
        first, count = SUBS[s]
        rows = pl.ds(first, count)
        for d in range(2):
            ring(2, d, s).wait_recv()
            ring(3, d, s).wait_recv()
        for h in range(2):
            fin[m, h, rows, :] = w[m, h, rows, :] + rsx[0, h, rows, :] + rsx[1, h, rows, :]
        for t in (4, 5):
            for d in range(2):
                ring(t, d, s).start()

    def pass_on(s):
        for d in range(2):
            ring(4, d, s).wait_recv()
            ring(6, d, s).start()

    def arrived(s):
        for d in range(2):
            ring(5, d, s).wait_recv()
            ring(6, d, s).wait_recv()

    own = jnp.concatenate([diag_ref[:32, :], diag_ref[32:, :]], axis=1)
    layer_diag[m] = own

    def diag_y(k):
        return pltpu.make_async_remote_copy(
            src_ref=layer_diag.at[m], dst_ref=layer_diag.at[m], send_sem=dy_send.at[k - 1], recv_sem=dy_recv.at[k - 1],
            device_id=(layer(k), r, c), device_id_type=MESH,
        )

    def diag_z(k):
        return pltpu.make_async_remote_copy(
            src_ref=grid_diag.at[c, r], dst_ref=grid_diag.at[c, r], send_sem=dz_send.at[k - 1], recv_sem=dz_recv.at[k - 1],
            device_id=(m, row_peer(k), c), device_id_type=MESH,
        )

    def diag_x(k):
        return pltpu.make_async_remote_copy(
            src_ref=grid_diag.at[c], dst_ref=grid_diag.at[c], send_sem=dx_send.at[k - 1], recv_sem=dx_recv.at[k - 1],
            device_id=(m, r, col_peer(k)), device_id_type=MESH,
        )

    for k in range(1, LAYERS):
        diag_y(k).start()

    load_column.wait()
    load_row.wait()
    for k in range(LAYERS):
        w[k, 0, 0:PANEL, :] = column_v[k * PANEL : (k + 1) * PANEL, :]
        w[k, 1, 0:PANEL, :] = row_v[k * PANEL : (k + 1) * PANEL, :]
    for t in (1, 2):
        for d in range(2):
            ring(t, d, 0).start()

    for k in range(1, LAYERS):
        diag_y(k).wait_recv()
    grid_diag[c, r] = layer_diag[0] + layer_diag[1] + layer_diag[2] + layer_diag[3]
    for k in range(1, grid_rows):
        diag_z(k).start()

    pattern = pattern_ref[...].astype(F32)
    weights[...] = jnp.concatenate(
        [jnp.broadcast_to(pattern[:, j : j + 1], (pattern.shape[0], BS)) for j in range(pattern.shape[1])], axis=1
    )

    def mask_front(k, h):
        load_front(k, h).wait()
        w[k, h, PANEL:HALF, :] = w[k, h, PANEL:HALF, :] * weights[pl.ds(k * 2 + h, 1), :]

    for k, h in order[:2]:
        mask_front(k, h)
    for s in range(1, len(SUBS)):
        for d in range(2):
            ring(1, d, s).start()
    for k, h in order[2:6]:
        mask_front(k, h)
    for s in range(1, len(SUBS)):
        for d in range(2):
            ring(2, d, s).start()
    add_opposite(0)
    for k in range(1, grid_rows):
        diag_z(k).wait_recv()
    for k in range(1, grid_cols):
        diag_x(k).start()
    for k, h in order[6:]:
        mask_front(k, h)
    finish_sum(0)
    pass_on(0)
    arrived(0)

    for k in range(LAYERS):
        all_columns[c, k * PANEL : (k + 1) * PANEL, :] = fin[k, 0, 0:PANEL, :]
        all_rows[r, k * PANEL : (k + 1) * PANEL, :] = fin[k, 1, 0:PANEL, :]

    def panel_z(k):
        return pltpu.make_async_remote_copy(
            src_ref=all_rows.at[r], dst_ref=all_rows.at[r], send_sem=pz_send.at[k - 1], recv_sem=pz_recv.at[k - 1],
            device_id=(m, row_peer(k), c), device_id_type=MESH,
        )

    def panel_x(k):
        return pltpu.make_async_remote_copy(
            src_ref=all_columns.at[c], dst_ref=all_columns.at[c], send_sem=px_send.at[k - 1], recv_sem=px_recv.at[k - 1],
            device_id=(m, r, col_peer(k)), device_id_type=MESH,
        )

    for k in range(1, grid_cols):
        diag_x(k).wait_recv()
    for k in range(1, grid_rows):
        panel_z(k).start()
    for k in range(1, grid_cols):
        panel_x(k).start()

    low = lax.broadcasted_iota(jnp.int32, (grid_rows, 32, 128), 2) < 64
    for pair in range(grid_cols // 2):
        left, right = grid_diag[2 * pair], grid_diag[2 * pair + 1]
        lanes = slice(pair * 128, (pair + 1) * 128)
        full_diag[:, 0, :, lanes] = jnp.where(low, left, pltpu.roll(right, 64, 2))
        full_diag[:, 1, :, lanes] = jnp.where(low, pltpu.roll(left, 64, 2), right)
    chosen = (lax.broadcasted_iota(jnp.int32, (width, width), 0) == pivot_ref[...]).astype(BF16)
    full = full_diag[...].reshape(width, width)
    parts = [contract(chosen, x, 0, 0) for x in split3(full)]
    a_ref[:, :width] = parts[0] + parts[1] + parts[2]
    a_ref[:, width:] = (
        lax.broadcasted_iota(jnp.int32, (width, width), 0) == lax.broadcasted_iota(jnp.int32, (width, width), 1)
    ).astype(F32)

    slots = {}
    for s in range(1, len(SUBS)):
        slots.setdefault((0, s - 1), []).append((add_opposite, s))
        slots.setdefault((1, s - 1), []).append((finish_sum, s))
    for s, slot in ((1, (2, 0)), (2, (2, 2)), (3, (3, 0)), (4, (3, 2))):
        slots.setdefault(slot, []).append((pass_on, s))

    def hook(i, at):
        for (block, place), work in slots.items():
            if place == at and block < blocks:
                @pl.when(i == block)
                def _(work=work):
                    for f, s in work:
                        f(s)

    @pl.loop(0, blocks)
    def _(i):
        eliminate_block(a_ref, d_ref, i, hook)

    for (block, place), work in sorted(slots.items()):
        if block >= blocks:
            for f, s in work:
                f(s)

    strip = a_ref[pl.ds(pl.multiple_of(c * 64, 64), 64), pl.ds(pl.multiple_of((r // 2) * 128, 128), 128)]
    odd = lax.rem(r, 2) == 1
    factor_v[...] = jnp.transpose(jnp.where(odd, pltpu.roll(strip, 64, 1), strip))[:64, :]
    store_factor = pltpu.make_async_copy(factor_v, factor_out, out_sem.at[0])
    store_factor.start()

    inverse = a_ref[:, width:]
    inv = split2(inverse)
    for k in range(1, grid_cols):
        panel_x(k).wait_recv()
    tile = 256

    def panel_tile(target, source, factor):
        @pl.loop(0, span // tile)
        def _(t):
            lanes = pl.ds(pl.multiple_of(t * tile, tile), tile)
            target[:, lanes] = dot3(factor, split2(source[:, :, lanes].reshape(width, tile)))

    panel_tile(left_x, all_columns, inv)
    store_lower = pltpu.make_async_copy(
        left_x.at[pl.ds(pl.multiple_of(c * 64, 64), 64), :], lower_out, out_sem.at[1]
    )
    store_lower.start()
    parts = [contract(x, chosen, 1, 1) for x in split3(inverse)]
    inv_pivot = split2(parts[0] + parts[1] + parts[2])
    for k in range(1, grid_rows):
        panel_z(k).wait_recv()
    panel_tile(right_x, all_rows, inv_pivot)
    store_upper = pltpu.make_async_copy(
        right_x.at[pl.ds(pl.multiple_of(r * 64, 64), 64), :], upper_out, out_sem.at[2]
    )
    store_upper.start()

    right = split2(right_x[...])

    @pl.loop(0, span // BS)
    def _(t):
        rows = pl.ds(pl.multiple_of(t * BS, BS), BS)
        update[t, :, :] = dot3(split2(jnp.transpose(left_x[:, rows])), right)

    def store_piece(k, h, s):
        first, count = SUBS[s]
        at = k * 2 * BS + h * BS + first - PANEL
        return pltpu.make_async_copy(
            update.at[k * 2 + h, pl.ds(first - PANEL, count), :],
            schur_out.at[pl.ds(at, count), :],
            out_sem.at[3 + (s - 1) * 8 + k * 2 + h],
        )

    for s in range(1, len(SUBS)):
        first, count = SUBS[s]
        rows = pl.ds(first, count)
        into = pl.ds(first - PANEL, count)
        arrived(s)
        for k in range(LAYERS):
            for h in range(2):
                update[k * 2 + h, into, :] = fin[k, h, rows, :] - update[k * 2 + h, into, :]
                store_piece(k, h, s).start()

    for s in range(len(SUBS)):
        for t in range(1, 7):
            for d in range(2):
                ring(t, d, s).wait_send()
    for k in range(1, LAYERS):
        diag_y(k).wait_send()
    for k in range(1, grid_rows):
        diag_z(k).wait_send()
        panel_z(k).wait_send()
    for k in range(1, grid_cols):
        diag_x(k).wait_send()
        panel_x(k).wait_send()
    store_factor.wait()
    store_lower.wait()
    store_upper.wait()
    for s in range(1, len(SUBS)):
        for k in range(LAYERS):
            for h in range(2):
                store_piece(k, h, s).wait()


def per_device(diag_parts, column_parts, row_parts, schur_parts, block_pattern, pivot_order):
    rows_dev, cols_dev = schur_parts.shape[1:]
    width = pivot_order.shape[0]
    grid_rows, grid_cols = lax.axis_size("row"), lax.axis_size("col")
    vmem = pl.BlockSpec(memory_space=pltpu.VMEM)
    anywhere = pl.BlockSpec(memory_space=pl.ANY)
    dma = pltpu.SemaphoreType.DMA
    subs = len(SUBS)
    factor, lower_t, upper, schur = pl.pallas_call(
        functools.partial(kernel, grid_rows, grid_cols),
        out_shape=(
            jax.ShapeDtypeStruct(diag_parts.shape[1:], F32),
            jax.ShapeDtypeStruct(column_parts.shape[:0:-1], F32),
            jax.ShapeDtypeStruct(row_parts.shape[1:], F32),
            jax.ShapeDtypeStruct(schur_parts.shape[1:], F32),
        ),
        in_specs=[vmem, vmem, vmem, anywhere, anywhere, anywhere],
        out_specs=[anywhere] * 4,
        scratch_shapes=[
            pltpu.VMEM((LAYERS, 2, HALF, cols_dev), F32),
            pltpu.VMEM((LAYERS, 2, HALF, cols_dev), F32),
            pltpu.VMEM((2, HALF, cols_dev), F32),
            pltpu.VMEM((2, 2, HALF, cols_dev), F32),
            pltpu.VMEM(column_parts.shape[:0:-1], F32),
            pltpu.VMEM(row_parts.shape[1:], F32),
            pltpu.VMEM(diag_parts.shape[1:], F32),
            pltpu.VMEM((rows_dev // BS, cols_dev), F32),
            pltpu.VMEM((LAYERS, 32, 128), F32),
            pltpu.VMEM((grid_cols, grid_rows, 32, 128), F32),
            pltpu.VMEM((grid_rows, 2, 32, width), F32),
            pltpu.VMEM((grid_cols, 64, rows_dev), F32),
            pltpu.VMEM((grid_rows, 64, cols_dev), F32),
            pltpu.VMEM((width, 2 * width), F32),
            pltpu.VMEM((128, 128), F32),
            pltpu.VMEM((width, rows_dev), F32),
            pltpu.VMEM((width, cols_dev), F32),
            pltpu.VMEM((rows_dev // BS, BS, cols_dev), F32),
            dma((10,)),
            dma((6, 2, subs)),
            dma((6, 2, subs)),
            dma((LAYERS - 1,)),
            dma((LAYERS - 1,)),
            dma((grid_rows - 1,)),
            dma((grid_rows - 1,)),
            dma((grid_cols - 1,)),
            dma((grid_cols - 1,)),
            dma((grid_rows - 1,)),
            dma((grid_rows - 1,)),
            dma((grid_cols - 1,)),
            dma((grid_cols - 1,)),
            dma((3 + (subs - 1) * 8,)),
        ],
        compiler_params=pltpu.CompilerParams(
            collective_id=0, has_side_effects=True, vmem_limit_bytes=56 << 20
        ),
    )(
        diag_parts[0],
        block_pattern[0],
        pivot_order.reshape(1, width),
        column_parts[0].T,
        row_parts[0],
        schur_parts[0],
    )
    return factor, lower_t.T, upper, schur


def solution(mesh):
    placed = (
        P("gz", "row", "col"),
        P("gz", "row", "col"),
        P("gz", "row", "col"),
        P("gz", "row", "col"),
        P("gz", "row", "col"),
        P(),
    )
    return jax.shard_map(
        per_device,
        mesh=mesh,
        in_specs=placed,
        out_specs=(P("row", "col"), P("row", "col"), P("row", "col"), P("row", "col")),
        check_vma=False,
    )
```

```python
import functools

import jax
import jax.numpy as jnp
from jax import lax
from jax.experimental import pallas as pl
from jax.experimental.pallas import tpu as pltpu
from jax.sharding import PartitionSpec as P

BS = 128
LAYERS = 4
PANEL = 16
HALF = PANEL + BS
SUBS = ((0, 16), (16, 32), (48, 32), (80, 32), (112, 32))
HI = lax.Precision.HIGHEST
F32 = jnp.float32
BF16 = jnp.bfloat16
MESH = pl.DeviceIdType.MESH


def split2(x):
    hi = x.astype(BF16)
    return hi, (x - hi.astype(F32)).astype(BF16)


def split3(x):
    hi = x.astype(BF16)
    rest = x - hi.astype(F32)
    mid = rest.astype(BF16)
    return hi, mid, (rest - mid.astype(F32)).astype(BF16)


def contract(a, b, da, db):
    return lax.dot_general(a, b, (((da,), (db,)), ((), ())), preferred_element_type=F32)


def dot3(a, b):
    return contract(a[0], b[0], 1, 0) + (contract(a[0], b[1], 1, 0) + contract(a[1], b[0], 1, 0))


def eliminate_group(d_ref, q):
    lane = lax.broadcasted_iota(jnp.int32, (8, 128), 1)
    sub = lax.broadcasted_iota(jnp.int32, (8, 128), 0)
    lo = 8 * q
    g = d_ref[lo : lo + 8, :]
    col = [jnp.broadcast_to(g[:, lo + j : lo + j + 1], (8, 128)) for j in range(8)]
    snap = jnp.zeros((8, 128), F32)
    pivots = jnp.ones((8, 128), F32)
    for k in range(8):
        piv = jnp.broadcast_to(col[k][k : k + 1, :], (8, 128))
        f = jnp.where(sub != k, col[k] * (1.0 / piv), 0.0)
        for j in range(k + 1, 8):
            col[j] = col[j] - f * jnp.broadcast_to(col[j][k : k + 1, :], (8, 128))
        g = jnp.where(lane == lo + k, jnp.where(sub == k, 1.0, 0.0), g)
        top = jnp.broadcast_to(g[k : k + 1, :], (8, 128))
        snap = jnp.where(sub == k, top, snap)
        pivots = jnp.where(sub == k, piv, pivots)
        g = g - f * top
    w = g / pivots
    if q < 15:
        n = 120 - lo
        below = d_ref[lo + 8 : 128, :]
        lane_b = lax.broadcasted_iota(jnp.int32, (n, 128), 1)
        acc = jnp.where((lane_b >= lo) & (lane_b < lo + 8), 0.0, below)
        for j in range(8):
            acc = acc - jnp.broadcast_to(below[:, lo + j : lo + j + 1], (n, 128)) * jnp.broadcast_to(
                w[j : j + 1, :], (n, 128)
            )
        d_ref[lo + 8 : 128, :] = acc
    d_ref[lo : lo + 8, :] = jnp.where(lane == lo + sub, 1.0, snap) * lax.rsqrt(pivots)
    return jnp.sqrt(pivots)


def eliminate_block(a_ref, d_ref, i, hook):
    width = a_ref.shape[0]
    at = pl.multiple_of(i * 128, 128)
    rows = pl.ds(at, 128)
    d_ref[...] = a_ref[rows, pl.ds(at, 128)]
    diagonal = []
    for q in range(16):
        if q % 4 == 0:
            hook(i, q // 4)
        diagonal.append(eliminate_group(d_ref, q))
    r = lax.broadcasted_iota(jnp.int32, (128, 128), 0)
    c = lax.broadcasted_iota(jnp.int32, (128, 128), 1)
    d = d_ref[...]
    inverse = jnp.where(c <= r, d, 0.0)
    upper = jnp.where(c > r, d, jnp.where(c == r, jnp.concatenate(diagonal, axis=0), 0.0))
    p = jnp.dot(inverse, a_ref[rows, :], precision=HI, preferred_element_type=F32)
    left = lax.broadcasted_iota(jnp.int32, (128, width), 1)
    right_of = jnp.where(left >= at + 128, p[:, :width], 0.0)
    a_ref[...] = a_ref[...] - lax.dot_general(
        right_of, p, (((0,), (0,)), ((), ())), precision=HI, preferred_element_type=F32
    )
    a_ref[rows, :] = jnp.concatenate([right_of, p[:, width:]], axis=1)
    a_ref[rows, pl.ds(at, 128)] = upper


def kernel(
    grid_rows, grid_cols,
    diag_hbm, pattern_hbm, pivot_hbm, column_ref, row_ref, schur_ref,
    factor_out, lower_out, upper_out, update,
    diag_ref, pattern_ref, pivot_ref, w, fin, rs1, rsx, column_v, row_v, weights,
    layer_diag, grid_diag, full_diag, all_columns, all_rows, a_ref, d_ref, left_x, right_x,
    load_sem, y_send, y_recv, dy_send, dy_recv, dz_send, dz_recv, dx_send, dx_recv, dc_send, dc_recv,
    pz_send, pz_recv, px_send, px_recv,
):
    m = lax.axis_index("gz")
    r = lax.axis_index("row")
    c = lax.axis_index("col")
    width = a_ref.shape[0]
    span = fin.shape[3]
    blocks = width // 128

    def layer(k):
        return lax.rem(m + k + LAYERS, LAYERS)

    def row_peer(k):
        return lax.rem(r + k + grid_rows, grid_rows)

    def col_peer(k):
        return lax.rem(c + k + grid_cols, grid_cols)

    small = [
        pltpu.make_async_copy(x, y, load_sem.at[10 + i])
        for i, (x, y) in enumerate(((diag_hbm, diag_ref), (pattern_hbm, pattern_ref), (pivot_hbm, pivot_ref)))
    ]
    for load in small:
        load.start()
    load_column = pltpu.make_async_copy(column_ref, column_v, load_sem.at[8])
    load_row = pltpu.make_async_copy(row_ref, row_v, load_sem.at[9])
    load_column.start()
    load_row.start()

    def load_front(k, h):
        block = k * 2 + h
        return pltpu.make_async_copy(
            schur_ref.at[pl.ds(pl.multiple_of(block * BS, BS), BS), :],
            w.at[k, h, pl.ds(PANEL, BS), :],
            load_sem.at[block],
        )

    order = [(layer(k), h) for k in (2, 1, -1, 0) for h in range(2)]
    for k, h in order:
        load_front(k, h).start()

    def ring(t, d, s):
        step = 1 - 2 * d
        to = layer(step)
        first, count = SUBS[s]
        rows = pl.ds(first, count)
        if t == 1:
            src, dst = w.at[layer(2), d, rows], rs1.at[d, rows]
        elif t == 2:
            src, dst = w.at[to, 1 - d, rows], rsx.at[d, 1 - d, rows]
        elif t == 3:
            src, dst = w.at[to, d, rows], rsx.at[d, d, rows]
        elif t == 4:
            src = dst = fin.at[m, d, rows]
        elif t == 5:
            src = dst = fin.at[m, 1 - d, rows]
        else:
            src = dst = fin.at[layer(-step), d, rows]
        return pltpu.make_async_remote_copy(
            src_ref=src, dst_ref=dst, send_sem=y_send.at[t - 1, d, s], recv_sem=y_recv.at[t - 1, d, s],
            device_id=(to, r, c), device_id_type=MESH,
        )

    def add_opposite(s):
        first, count = SUBS[s]
        rows = pl.ds(first, count)
        for d in range(2):
            ring(1, d, s).wait_recv()
            to = layer(1 - 2 * d)
            w[to, d, rows, :] = w[to, d, rows, :] + rs1[d, rows, :]
            ring(3, d, s).start()

    def finish_sum(s):
        first, count = SUBS[s]
        rows = pl.ds(first, count)
        for d in range(2):
            ring(2, d, s).wait_recv()
            ring(3, d, s).wait_recv()
        for h in range(2):
            fin[m, h, rows, :] = w[m, h, rows, :] + rsx[0, h, rows, :] + rsx[1, h, rows, :]
        for t in (4, 5):
            for d in range(2):
                ring(t, d, s).start()

    def pass_on(s):
        for d in range(2):
            ring(4, d, s).wait_recv()
            ring(6, d, s).start()

    def arrived(s):
        for d in range(2):
            ring(5, d, s).wait_recv()
            ring(6, d, s).wait_recv()

    def diag_y(k):
        return pltpu.make_async_remote_copy(
            src_ref=layer_diag.at[m], dst_ref=layer_diag.at[m], send_sem=dy_send.at[k - 1], recv_sem=dy_recv.at[k - 1],
            device_id=(layer(k), r, c), device_id_type=MESH,
        )

    def diag_z(k):
        return pltpu.make_async_remote_copy(
            src_ref=grid_diag.at[c, r], dst_ref=grid_diag.at[c, r], send_sem=dz_send.at[k - 1], recv_sem=dz_recv.at[k - 1],
            device_id=(m, row_peer(k), c), device_id_type=MESH,
        )

    def diag_x(j):
        ref = grid_diag.at[c]
        return pltpu.make_async_remote_copy(
            src_ref=ref, dst_ref=ref, send_sem=dx_send.at[j - 1], recv_sem=dx_recv.at[j - 1],
            device_id=(m, r, col_peer(2 * j)), device_id_type=MESH,
        )

    def diag_core(j):
        ref = grid_diag.at[col_peer(-2 * j)]
        return pltpu.make_async_remote_copy(
            src_ref=ref, dst_ref=ref, send_sem=dc_send.at[j], recv_sem=dc_recv.at[j],
            device_id=(m, r, c + 1 - 2 * lax.rem(c, 2)), device_id_type=MESH,
        )

    barrier = pltpu.get_barrier_semaphore()
    for k in range(1, LAYERS):
        pl.semaphore_signal(barrier, inc=1, device_id=(layer(k), r, c), device_id_type=MESH)
    for k in range(1, grid_rows):
        pl.semaphore_signal(barrier, inc=1, device_id=(m, row_peer(k), c), device_id_type=MESH)
    for k in range(1, grid_cols):
        pl.semaphore_signal(barrier, inc=1, device_id=(m, r, col_peer(k)), device_id_type=MESH)

    for load in small:
        load.wait()
    own = jnp.concatenate([diag_ref[:32, :], diag_ref[32:, :]], axis=1)
    layer_diag[m] = own
    pattern = pattern_ref[...].astype(F32)
    weights[...] = jnp.concatenate(
        [jnp.broadcast_to(pattern[:, j : j + 1], (pattern.shape[0], BS)) for j in range(pattern.shape[1])], axis=1
    )

    def mask_front(k, h):
        load_front(k, h).wait()
        w[k, h, PANEL:HALF, :] = w[k, h, PANEL:HALF, :] * weights[pl.ds(k * 2 + h, 1), :]

    def send(t, s):
        for d in range(2):
            ring(t, d, s).start()

    load_column.wait()
    load_row.wait()
    for k in range(LAYERS):
        w[k, 0, 0:PANEL, :] = column_v[k * PANEL : (k + 1) * PANEL, :]
        w[k, 1, 0:PANEL, :] = row_v[k * PANEL : (k + 1) * PANEL, :]
    pl.semaphore_wait(barrier, LAYERS - 1 + grid_rows - 1 + grid_cols - 1)

    for k in range(1, LAYERS):
        diag_y(k).start()
    send(1, 0)
    send(2, 0)
    for k, h in order[:2]:
        mask_front(k, h)
    send(1, 1)
    for k in range(1, LAYERS):
        diag_y(k).wait_recv()
    grid_diag[c, r] = layer_diag[0] + layer_diag[1] + layer_diag[2] + layer_diag[3]
    for k in range(1, grid_rows):
        diag_z(k).start()
    add_opposite(0)
    send(1, 2)
    for k, h in order[2:6]:
        mask_front(k, h)
    for k in range(1, grid_rows):
        diag_z(k).wait_recv()
    diag_core(0).start()
    for j in range(1, grid_cols // 2):
        diag_x(j).start()
    for k, h in order[6:]:
        mask_front(k, h)
    finish_sum(0)
    send(1, 3)
    pass_on(0)
    send(1, 4)
    for s in range(1, len(SUBS)):
        send(2, s)

    far = grid_rows // 2

    def panel_z(j, d):
        step = 1 - 2 * d
        block = row_peer(-step * j)
        ref = all_rows.at[block, pl.ds(32 * d, 32)] if j == far - 1 else all_rows.at[block]
        return pltpu.make_async_remote_copy(
            src_ref=ref, dst_ref=ref, send_sem=pz_send.at[j, d], recv_sem=pz_recv.at[j, d],
            device_id=(m, row_peer(step), c), device_id_type=MESH,
        )

    def panel_x(k):
        return pltpu.make_async_remote_copy(
            src_ref=all_columns.at[c], dst_ref=all_columns.at[c], send_sem=px_send.at[k - 1], recv_sem=px_recv.at[k - 1],
            device_id=(m, r, col_peer(k)), device_id_type=MESH,
        )

    def spread_panels(s):
        arrived(s)
        for k in range(LAYERS):
            all_columns[c, k * PANEL : (k + 1) * PANEL, :] = fin[k, 0, 0:PANEL, :]
            all_rows[r, k * PANEL : (k + 1) * PANEL, :] = fin[k, 1, 0:PANEL, :]
        for d in range(2):
            panel_z(0, d).start()
        for k in range(1, grid_cols):
            panel_x(k).start()

    def rows_on(j):
        for d in range(2):
            panel_z(j - 1, d).wait_recv()
            panel_z(j, d).start()

    for j in range(1, grid_cols // 2):
        diag_x(j).wait_recv()
        diag_core(j).start()
    for j in range(grid_cols // 2):
        diag_core(j).wait_recv()

    low = lax.broadcasted_iota(jnp.int32, (grid_rows, 32, 128), 2) < 64
    for pair in range(grid_cols // 2):
        left, right = grid_diag[2 * pair], grid_diag[2 * pair + 1]
        lanes = slice(pair * 128, (pair + 1) * 128)
        full_diag[:, 0, :, lanes] = jnp.where(low, left, pltpu.roll(right, 64, 2))
        full_diag[:, 1, :, lanes] = jnp.where(low, pltpu.roll(left, 64, 2), right)
    chosen = (lax.broadcasted_iota(jnp.int32, (width, width), 0) == pivot_ref[...]).astype(BF16)
    full = full_diag[...].reshape(width, width)
    parts = [contract(chosen, x, 0, 0) for x in split3(full)]
    a_ref[:, :width] = parts[0] + parts[1] + parts[2]
    a_ref[:, width:] = (
        lax.broadcasted_iota(jnp.int32, (width, width), 0) == lax.broadcasted_iota(jnp.int32, (width, width), 1)
    ).astype(F32)

    slots = {
        (0, 1): [(add_opposite, 1), (add_opposite, 2), (add_opposite, 3)],
        (0, 3): [(spread_panels, 0), (add_opposite, 4)],
        (1, 2): [(rows_on, 1)],
        (2, 1): [(rows_on, 2)],
        (2, 2): [(finish_sum, 1)],
        (2, 3): [(finish_sum, 2)],
        (3, 0): [(finish_sum, 3), (rows_on, 3)],
        (3, 1): [(finish_sum, 4)],
        (5, 0): [(pass_on, 1), (pass_on, 2)],
    }
    slots = {at: [(f, s) for f, s in work if f is not rows_on or s < far] for at, work in slots.items()}

    def hook(i, at):
        for (block, place), work in slots.items():
            if place == at and block < blocks and work:
                @pl.when(i == block)
                def _(work=work):
                    for f, s in work:
                        f(s)

    def hooks_after(least, most):
        for (block, place), work in sorted(slots.items()):
            if least <= block <= most:
                for f, s in work:
                    f(s)

    @pl.loop(0, blocks)
    def _(i):
        eliminate_block(a_ref, d_ref, i, hook)

    hooks_after(blocks, 4)

    strip = a_ref[pl.ds(pl.multiple_of(c * 64, 64), 64), pl.ds(pl.multiple_of((r // 2) * 128, 128), 128)]
    odd = lax.rem(r, 2) == 1
    factor_out[...] = jnp.transpose(jnp.where(odd, pltpu.roll(strip, 64, 1), strip))[:64, :]

    inverse = a_ref[:, width:]
    inv = split2(inverse)
    for k in range(1, grid_cols):
        panel_x(k).wait_recv()
    tile = 256

    def panel_tile(target, source, factor):
        @pl.loop(0, span // tile)
        def _(t):
            lanes = pl.ds(pl.multiple_of(t * tile, tile), tile)
            target[:, lanes] = dot3(factor, split2(source[:, :, lanes].reshape(width, tile)))

    panel_tile(left_x, all_columns, inv)
    lower_out[...] = left_x[pl.ds(pl.multiple_of(c * 64, 64), 64), :]
    parts = [contract(x, chosen, 1, 1) for x in split3(inverse)]
    inv_pivot = split2(parts[0] + parts[1] + parts[2])
    for d in range(2):
        panel_z(far - 1, d).wait_recv()
    panel_tile(right_x, all_rows, inv_pivot)
    upper_out[...] = right_x[pl.ds(pl.multiple_of(r * 64, 64), 64), :]

    right = split2(right_x[...])

    @pl.loop(0, span // BS)
    def _(t):
        rows = pl.ds(pl.multiple_of(t * BS, BS), BS)
        update[t, :, :] = dot3(split2(jnp.transpose(left_x[:, rows])), right)

    def subtract(k, h, s):
        first, count = SUBS[s]
        into = pl.ds(first - PANEL, count)
        update[k * 2 + h, into, :] = fin[k, h, pl.ds(first, count), :] - update[k * 2 + h, into, :]

    hooks_after(5, 5)
    for s in range(1, len(SUBS)):
        for h in range(2):
            subtract(m, h, s)
    for s in range(1, len(SUBS)):
        if s > 2:
            pass_on(s)
        for d in range(2):
            ring(5, d, s).wait_recv()
        for k in (1, -1):
            for h in range(2):
                subtract(layer(k), h, s)
    for s in range(1, len(SUBS)):
        for d in range(2):
            ring(6, d, s).wait_recv()
        for h in range(2):
            subtract(layer(2), h, s)

    for s in range(len(SUBS)):
        for t in range(1, 7):
            for d in range(2):
                ring(t, d, s).wait_send()
    for k in range(1, LAYERS):
        diag_y(k).wait_send()
    for k in range(1, grid_rows):
        diag_z(k).wait_send()
    for k in range(1, grid_cols):
        panel_x(k).wait_send()
    for j in range(far):
        for d in range(2):
            panel_z(j, d).wait_send()
    for j in range(grid_cols // 2):
        diag_core(j).wait_send()
        if j:
            diag_x(j).wait_send()

def store_kernel(*refs):
    ins, outs, sem = refs[:4], refs[4:8], refs[8]
    copies = [pltpu.make_async_copy(x, y, sem.at[i]) for i, (x, y) in enumerate(zip(ins, outs))]
    for copy in copies[::-1]:
        copy.start()
    for copy in copies:
        copy.wait()


def per_device(diag_parts, column_parts, row_parts, schur_parts, block_pattern, pivot_order):
    rows_dev, cols_dev = schur_parts.shape[1:]
    width = pivot_order.shape[0]
    grid_rows, grid_cols = lax.axis_size("row"), lax.axis_size("col")
    vmem = pl.BlockSpec(memory_space=pltpu.VMEM)
    anywhere = pl.BlockSpec(memory_space=pl.ANY)
    dma = pltpu.SemaphoreType.DMA
    subs = len(SUBS)
    shapes = (
        diag_parts.shape[1:],
        column_parts.shape[:0:-1],
        row_parts.shape[1:],
        (rows_dev // BS, BS, cols_dev),
    )
    held = pl.pallas_call(
        functools.partial(kernel, grid_rows, grid_cols),
        out_shape=tuple(pltpu.VMEM(shape, F32) for shape in shapes),
        in_specs=[pl.BlockSpec(memory_space=pltpu.HBM)] * 6,
        out_specs=[vmem] * 4,
        scratch_shapes=[
            pltpu.VMEM(diag_parts.shape[1:], F32),
            pltpu.VMEM(block_pattern.shape[1:], jnp.int32),
            pltpu.VMEM((1, width), jnp.int32),
            pltpu.VMEM((LAYERS, 2, HALF, cols_dev), F32),
            pltpu.VMEM((LAYERS, 2, HALF, cols_dev), F32),
            pltpu.VMEM((2, HALF, cols_dev), F32),
            pltpu.VMEM((2, 2, HALF, cols_dev), F32),
            pltpu.VMEM(column_parts.shape[:0:-1], F32),
            pltpu.VMEM(row_parts.shape[1:], F32),
            pltpu.VMEM((rows_dev // BS, cols_dev), F32),
            pltpu.VMEM((LAYERS, 32, 128), F32),
            pltpu.VMEM((grid_cols, grid_rows, 32, 128), F32),
            pltpu.VMEM((grid_rows, 2, 32, width), F32),
            pltpu.VMEM((grid_cols, 64, rows_dev), F32),
            pltpu.VMEM((grid_rows, 64, cols_dev), F32),
            pltpu.VMEM((width, 2 * width), F32),
            pltpu.VMEM((128, 128), F32),
            pltpu.VMEM((width, rows_dev), F32),
            pltpu.VMEM((width, cols_dev), F32),
            dma((13,)),
            dma((6, 2, subs)),
            dma((6, 2, subs)),
            dma((LAYERS - 1,)),
            dma((LAYERS - 1,)),
            dma((grid_rows - 1,)),
            dma((grid_rows - 1,)),
            dma((max(grid_cols // 2 - 1, 1),)),
            dma((max(grid_cols // 2 - 1, 1),)),
            dma((grid_cols // 2,)),
            dma((grid_cols // 2,)),
            dma((grid_rows // 2, 2)),
            dma((grid_rows // 2, 2)),
            dma((grid_cols - 1,)),
            dma((grid_cols - 1,)),
        ],
        compiler_params=pltpu.CompilerParams(
            collective_id=0, has_side_effects=True, vmem_limit_bytes=48 << 20
        ),
    )(
        *(
            pltpu.with_memory_space_constraint(x, pltpu.HBM)
            for x in (
                diag_parts[0],
                block_pattern[0],
                pivot_order.reshape(1, width),
                column_parts[0].T,
                row_parts[0],
                schur_parts[0],
            )
        )
    )
    factor, lower_t, upper, schur = pl.pallas_call(
        store_kernel,
        out_shape=tuple(jax.ShapeDtypeStruct(shape, F32) for shape in shapes),
        in_specs=[vmem] * 4,
        out_specs=[anywhere] * 4,
        scratch_shapes=[dma((4,))],
        compiler_params=pltpu.CompilerParams(vmem_limit_bytes=8 << 20),
    )(*held)
    return factor, lower_t.T, upper, schur.reshape(rows_dev, cols_dev)


def solution(mesh):
    placed = (
        P("gz", "row", "col"),
        P("gz", "row", "col"),
        P("gz", "row", "col"),
        P("gz", "row", "col"),
        P("gz", "row", "col"),
        P(),
    )
    return jax.shard_map(
        per_device,
        mesh=mesh,
        in_specs=placed,
        out_specs=(P("row", "col"), P("row", "col"), P("row", "col"), P("row", "col")),
        check_vma=False,
    )
```

```python
import functools

import jax
import jax.numpy as jnp
from jax import lax
from jax.experimental import pallas as pl
from jax.experimental.pallas import tpu as pltpu
from jax.sharding import PartitionSpec as P

BS = 128
LAYERS = 4
PANEL = 16
HALF = PANEL + BS
SUBS = ((0, 16), (16, 32), (48, 32), (80, 32), (112, 32))
HI = lax.Precision.HIGHEST
F32 = jnp.float32
BF16 = jnp.bfloat16
MESH = pl.DeviceIdType.MESH


def split2(x):
    hi = x.astype(BF16)
    return hi, (x - hi.astype(F32)).astype(BF16)


def split3(x):
    hi = x.astype(BF16)
    rest = x - hi.astype(F32)
    mid = rest.astype(BF16)
    return hi, mid, (rest - mid.astype(F32)).astype(BF16)


def contract(a, b, da, db):
    return lax.dot_general(a, b, (((da,), (db,)), ((), ())), preferred_element_type=F32)


def dot3(a, b):
    return contract(a[0], b[0], 1, 0) + (contract(a[0], b[1], 1, 0) + contract(a[1], b[0], 1, 0))


def eliminate_group(d_ref, q):
    lane = lax.broadcasted_iota(jnp.int32, (8, 128), 1)
    sub = lax.broadcasted_iota(jnp.int32, (8, 128), 0)
    lo = 8 * q
    g = d_ref[lo : lo + 8, :]
    col = [jnp.broadcast_to(g[:, lo + j : lo + j + 1], (8, 128)) for j in range(8)]
    snap = jnp.zeros((8, 128), F32)
    pivots = jnp.ones((8, 128), F32)
    for k in range(8):
        piv = jnp.broadcast_to(col[k][k : k + 1, :], (8, 128))
        f = jnp.where(sub != k, col[k] * (1.0 / piv), 0.0)
        for j in range(k + 1, 8):
            col[j] = col[j] - f * jnp.broadcast_to(col[j][k : k + 1, :], (8, 128))
        g = jnp.where(lane == lo + k, jnp.where(sub == k, 1.0, 0.0), g)
        top = jnp.broadcast_to(g[k : k + 1, :], (8, 128))
        snap = jnp.where(sub == k, top, snap)
        pivots = jnp.where(sub == k, piv, pivots)
        g = g - f * top
    w = g / pivots
    if q < 15:
        below = d_ref[lo + 8 : lo + 16, :]
        acc = jnp.where((lane >= lo) & (lane < lo + 8), 0.0, below)
        for j in range(8):
            acc = acc - jnp.broadcast_to(below[:, lo + j : lo + j + 1], (8, 128)) * jnp.broadcast_to(
                w[j : j + 1, :], (8, 128)
            )
        d_ref[lo + 8 : lo + 16, :] = acc
    if q < 14:
        gh, gm, gl = (x.astype(F32) for x in split3(d_ref[lo : lo + 8, :]))
        wh, wm, wl = (x.astype(F32) for x in split3(w))
        update = contract(
            jnp.concatenate([gh, gh, gm, gh, gm, gl], axis=0).astype(BF16),
            jnp.concatenate([wh, wm, wh, wl, wm, wh], axis=0).astype(BF16),
            0,
            0,
        )
        rest = d_ref[lo + 16 : 128, :]
        lane_r = lax.broadcasted_iota(jnp.int32, rest.shape, 1)
        d_ref[lo + 16 : 128, :] = jnp.where((lane_r >= lo) & (lane_r < lo + 8), 0.0, rest) - update[lo + 16 :, :]
    d_ref[lo : lo + 8, :] = jnp.where(lane == lo + sub, 1.0, snap) * lax.rsqrt(pivots)
    return jnp.sqrt(pivots)


def eliminate_block(a_ref, d_ref, up_ref, i, hook):
    width = a_ref.shape[0]
    at = pl.multiple_of(i * 128, 128)
    rows = pl.ds(at, 128)
    d_ref[...] = a_ref[rows, pl.ds(at, 128)]
    diagonal = []
    for q in range(16):
        if q % 4 == 0:
            hook(i, q // 4)
        diagonal.append(eliminate_group(d_ref, q))
    r = lax.broadcasted_iota(jnp.int32, (128, 128), 0)
    c = lax.broadcasted_iota(jnp.int32, (128, 128), 1)
    d = d_ref[...]
    inverse = jnp.where(c <= r, d, 0.0)
    upper = jnp.where(c > r, d, jnp.where(c == r, jnp.concatenate(diagonal, axis=0), 0.0))
    up_ref[i] = upper
    a_ref[rows, :] = jnp.dot(inverse, a_ref[rows, :], precision=HI, preferred_element_type=F32)
    a_ref[rows, pl.ds(at, 128)] = inverse

    @pl.loop(i + 1, width // 128)
    def _(j):
        below = pl.ds(pl.multiple_of(j * 128, 128), 128)
        a_ref[below, pl.ds(at, 128)] = jnp.zeros((128, 128), F32)
        a_ref[below, :] = a_ref[below, :] - lax.dot_general(
            a_ref[rows, below], a_ref[rows, :], (((0,), (0,)), ((), ())), precision=HI, preferred_element_type=F32
        )


def kernel(
    grid_rows, grid_cols,
    diag_hbm, pattern_hbm, pivot_hbm, column_ref, row_ref, schur_ref,
    factor_out, lower_out, upper_out, update,
    diag_ref, pattern_ref, pivot_ref, w, fin, rs1, rsx, column_v, row_v, weights,
    layer_diag, grid_diag, full_diag, all_columns, all_rows, a_ref, d_ref, up_ref, left_x, right_x,
    load_sem, y_send, y_recv, dy_send, dy_recv, dz_send, dz_recv, dx_send, dx_recv, dc_send, dc_recv,
    pz_send, pz_recv, px_send, px_recv, pc_send, pc_recv,
):
    m = lax.axis_index("gz")
    r = lax.axis_index("row")
    c = lax.axis_index("col")
    width = a_ref.shape[0]
    span = fin.shape[3]
    blocks = width // 128

    def layer(k):
        return lax.rem(m + k + LAYERS, LAYERS)

    def row_peer(k):
        return lax.rem(r + k + grid_rows, grid_rows)

    def col_peer(k):
        return lax.rem(c + k + grid_cols, grid_cols)

    small = [
        pltpu.make_async_copy(x, y, load_sem.at[10 + i])
        for i, (x, y) in enumerate(((diag_hbm, diag_ref), (pattern_hbm, pattern_ref), (pivot_hbm, pivot_ref)))
    ]
    for load in small:
        load.start()
    load_column = pltpu.make_async_copy(column_ref, column_v, load_sem.at[8])
    load_row = pltpu.make_async_copy(row_ref, row_v, load_sem.at[9])
    load_column.start()
    load_row.start()

    def load_front(k, h):
        block = k * 2 + h
        return pltpu.make_async_copy(
            schur_ref.at[pl.ds(pl.multiple_of(block * BS, BS), BS), :],
            w.at[k, h, pl.ds(PANEL, BS), :],
            load_sem.at[block],
        )

    order = [(layer(k), h) for k in (2, 1, -1, 0) for h in range(2)]
    for k, h in order:
        load_front(k, h).start()

    def ring(t, d, s):
        step = 1 - 2 * d
        to = layer(step)
        first, count = SUBS[s]
        rows = pl.ds(first, count)
        if t == 1:
            src, dst = w.at[layer(2), d, rows], rs1.at[d, rows]
        elif t == 2:
            src, dst = w.at[to, 1 - d, rows], rsx.at[d, 1 - d, rows]
        elif t == 3:
            src, dst = w.at[to, d, rows], rsx.at[d, d, rows]
        elif t == 4:
            src = dst = fin.at[m, d, rows]
        elif t == 5:
            src = dst = fin.at[m, 1 - d, rows]
        else:
            src = dst = fin.at[layer(-step), d, rows]
        return pltpu.make_async_remote_copy(
            src_ref=src, dst_ref=dst, send_sem=y_send.at[t - 1, d, s], recv_sem=y_recv.at[t - 1, d, s],
            device_id=(to, r, c), device_id_type=MESH,
        )

    def add_opposite(s):
        first, count = SUBS[s]
        rows = pl.ds(first, count)
        for d in range(2):
            ring(1, d, s).wait_recv()
            to = layer(1 - 2 * d)
            w[to, d, rows, :] = w[to, d, rows, :] + rs1[d, rows, :]
            ring(3, d, s).start()

    def finish_sum(s):
        first, count = SUBS[s]
        rows = pl.ds(first, count)
        for d in range(2):
            ring(2, d, s).wait_recv()
            ring(3, d, s).wait_recv()
        for h in range(2):
            fin[m, h, rows, :] = w[m, h, rows, :] + rsx[0, h, rows, :] + rsx[1, h, rows, :]
        for t in (4, 5):
            for d in range(2):
                ring(t, d, s).start()

    def pass_on(s):
        for d in range(2):
            ring(4, d, s).wait_recv()
            ring(6, d, s).start()

    def arrived(s):
        for d in range(2):
            ring(5, d, s).wait_recv()
            ring(6, d, s).wait_recv()

    def diag_y(k):
        return pltpu.make_async_remote_copy(
            src_ref=layer_diag.at[m], dst_ref=layer_diag.at[m], send_sem=dy_send.at[k - 1], recv_sem=dy_recv.at[k - 1],
            device_id=(layer(k), r, c), device_id_type=MESH,
        )

    stages = [[k for k in stage if k < grid_rows] for stage in ((1,), (2,), (3, 4), (5, 6, 7))]

    def along_z(k, act):
        for d in range(2):
            to = r + k * (1 - 2 * d)
            copy = pltpu.make_async_remote_copy(
                src_ref=grid_diag.at[c, r], dst_ref=grid_diag.at[c, r],
                send_sem=dz_send.at[k - 1, d], recv_sem=dz_recv.at[k - 1, d],
                device_id=(m, lax.rem(to + grid_rows, grid_rows), c), device_id_type=MESH,
            )
            ahead, behind = to < grid_rows, to >= 0
            if act == "recv":
                ahead, behind = r - k * (1 - 2 * d) < grid_rows, r - k * (1 - 2 * d) >= 0

            @pl.when(jnp.logical_and(ahead, behind))
            def _(copy=copy):
                if act == "start":
                    copy.start()
                elif act == "recv":
                    copy.wait_recv()
                else:
                    copy.wait_send()

    def stage_z(i, act):
        for k in stages[i]:
            along_z(k, act)

    class AlongX:
        def __init__(self, ref, sems):
            self.ref, self.sems, self.steps = ref, sems, grid_cols // 4

        def part(self, j, d):
            block = col_peer(2 * j * (2 * d - 1))
            if j == self.steps - 1:
                half = self.ref.shape[1] // 2
                return self.ref.at[block, pl.ds(half * d, half)]
            return self.ref.at[block]

        def chip(self, j, d):
            ref = self.part(j, d)
            return pltpu.make_async_remote_copy(
                src_ref=ref, dst_ref=ref, send_sem=self.sems[0].at[j, d], recv_sem=self.sems[1].at[j, d],
                device_id=(m, r, col_peer(2 - 4 * d)), device_id_type=MESH,
            )

        def core(self, i):
            if i == 0:
                ref = self.ref.at[c]
            else:
                j, d = divmod(i - 1, 2)
                block = col_peer(2 * (j + 1) * (2 * d - 1))
                ref = self.ref.at[block]
                if j == self.steps - 1:
                    half = self.ref.shape[1] // 2
                    ref = self.ref.at[block, pl.ds(half * d, half)]
            return pltpu.make_async_remote_copy(
                src_ref=ref, dst_ref=ref, send_sem=self.sems[2].at[i], recv_sem=self.sems[3].at[i],
                device_id=(m, r, c + 1 - 2 * lax.rem(c, 2)), device_id_type=MESH,
            )

        def start(self):
            for d in range(2):
                if self.steps:
                    self.chip(0, d).start()
            self.core(0).start()

        def go_on(self, j):
            for d in range(2):
                self.chip(j, d).wait_recv()
                if j + 1 < self.steps:
                    self.chip(j + 1, d).start()
                self.core(1 + 2 * j + d).start()

        def finish(self):
            for i in range(1 + 2 * self.steps):
                self.core(i).wait_recv()

        def drain(self):
            for i in range(1 + 2 * self.steps):
                self.core(i).wait_send()
            for j in range(self.steps):
                for d in range(2):
                    self.chip(j, d).wait_send()

    diag_x = AlongX(grid_diag, (dx_send, dx_recv, dc_send, dc_recv))
    panel_x = AlongX(all_columns, (px_send, px_recv, pc_send, pc_recv))

    barrier = pltpu.get_barrier_semaphore()
    for k in range(1, LAYERS):
        pl.semaphore_signal(barrier, inc=1, device_id=(layer(k), r, c), device_id_type=MESH)
    for step in (1, -1):
        @pl.when(jnp.logical_and(r + step >= 0, r + step < grid_rows))
        def _(step=step):
            pl.semaphore_signal(barrier, inc=1, device_id=(m, row_peer(step), c), device_id_type=MESH)
    for k in range(1, grid_cols):
        pl.semaphore_signal(barrier, inc=1, device_id=(m, r, col_peer(k)), device_id_type=MESH)

    for load in small:
        load.wait()
    own = jnp.concatenate([diag_ref[:32, :], diag_ref[32:, :]], axis=1)
    layer_diag[m] = own
    pattern = pattern_ref[...].astype(F32)
    weights[...] = jnp.concatenate(
        [jnp.broadcast_to(pattern[:, j : j + 1], (pattern.shape[0], BS)) for j in range(pattern.shape[1])], axis=1
    )

    def mask_front(k, h):
        load_front(k, h).wait()
        w[k, h, PANEL:HALF, :] = w[k, h, PANEL:HALF, :] * weights[pl.ds(k * 2 + h, 1), :]

    def send(t, s):
        for d in range(2):
            ring(t, d, s).start()

    load_column.wait()
    load_row.wait()
    for k in range(LAYERS):
        w[k, 0, 0:PANEL, :] = column_v[k * PANEL : (k + 1) * PANEL, :]
        w[k, 1, 0:PANEL, :] = row_v[k * PANEL : (k + 1) * PANEL, :]
    ends = jnp.where(r == 0, 1, 0) + jnp.where(r == grid_rows - 1, 1, 0)
    pl.semaphore_wait(barrier, LAYERS - 1 + 2 - ends + grid_cols - 1)

    for k in range(1, LAYERS):
        diag_y(k).start()
    send(1, 0)
    send(2, 0)
    for k, h in order[:2]:
        mask_front(k, h)
    send(1, 1)
    for k in range(1, LAYERS):
        diag_y(k).wait_recv()
    grid_diag[c, r] = layer_diag[0] + layer_diag[1] + layer_diag[2] + layer_diag[3]
    stage_z(0, "start")
    add_opposite(0)
    send(1, 2)
    for k, h in order[2:6]:
        mask_front(k, h)
    stage_z(0, "recv")
    stage_z(1, "start")
    finish_sum(0)
    send(1, 3)
    stage_z(1, "recv")
    stage_z(2, "start")
    pass_on(0)
    send(1, 4)
    for s in range(1, len(SUBS)):
        send(2, s)
    for k, h in order[6:]:
        mask_front(k, h)
    stage_z(2, "recv")
    stage_z(3, "start")
    stage_z(3, "recv")
    diag_x.start()

    far = grid_rows // 2

    def panel_z(j, d):
        step = 1 - 2 * d
        block = row_peer(-step * j)
        ref = all_rows.at[block, pl.ds(32 * d, 32)] if j == far - 1 else all_rows.at[block]
        return pltpu.make_async_remote_copy(
            src_ref=ref, dst_ref=ref, send_sem=pz_send.at[j, d], recv_sem=pz_recv.at[j, d],
            device_id=(m, row_peer(step), c), device_id_type=MESH,
        )

    def spread_panels(s):
        arrived(s)
        for k in range(LAYERS):
            all_columns[c, k * PANEL : (k + 1) * PANEL, :] = fin[k, 0, 0:PANEL, :]
            all_rows[r, k * PANEL : (k + 1) * PANEL, :] = fin[k, 1, 0:PANEL, :]
        for d in range(2):
            panel_z(0, d).start()
        panel_x.start()

    def rows_on(j):
        for d in range(2):
            panel_z(j - 1, d).wait_recv()
            panel_z(j, d).start()

    def columns_on(j):
        panel_x.go_on(j)

    add_opposite(1)
    add_opposite(2)
    for j in range(diag_x.steps):
        diag_x.go_on(j)
    spread_panels(0)
    add_opposite(3)
    add_opposite(4)
    diag_x.finish()

    low = lax.broadcasted_iota(jnp.int32, (grid_rows, 32, 128), 2) < 64
    for pair in range(grid_cols // 2):
        left, right = grid_diag[2 * pair], grid_diag[2 * pair + 1]
        lanes = slice(pair * 128, (pair + 1) * 128)
        full_diag[:, 0, :, lanes] = jnp.where(low, left, pltpu.roll(right, 64, 2))
        full_diag[:, 1, :, lanes] = jnp.where(low, pltpu.roll(left, 64, 2), right)
    chosen = (lax.broadcasted_iota(jnp.int32, (width, width), 0) == pivot_ref[...]).astype(BF16)
    full = full_diag[...].reshape(width, width)
    parts = [contract(chosen, x, 0, 0) for x in split3(full)]
    a_ref[...] = parts[0] + parts[1] + parts[2]

    slots = {
        (0, 0): [(finish_sum, 1)],
        (0, 1): [(rows_on, 1), (columns_on, 0)],
        (0, 3): [(finish_sum, 2)],
        (1, 1): [(finish_sum, 3), (columns_on, 1)],
        (1, 3): [(rows_on, 2)],
        (2, 0): [(finish_sum, 4)],
        (2, 3): [(rows_on, 3)],
        (3, 2): [(pass_on, 1)],
    }
    slots = {at: [
            (f, s) for f, s in work if not (f is rows_on and s >= far) and not (f is columns_on and s >= panel_x.steps)
        ]
        for at, work in slots.items()}

    def hook(i, at):
        for (block, place), work in slots.items():
            if place == at and block < blocks and work:
                @pl.when(i == block)
                def _(work=work):
                    for f, s in work:
                        f(s)

    def hooks_after(least, most):
        for (block, place), work in sorted(slots.items()):
            if least <= block <= most:
                for f, s in work:
                    f(s)

    @pl.loop(0, blocks)
    def _(i):
        eliminate_block(a_ref, d_ref, up_ref, i, hook)

    hooks_after(blocks, 4)

    strip = a_ref[pl.ds(pl.multiple_of(c * 64, 64), 64), pl.ds(pl.multiple_of((r // 2) * 128, 128), 128)]
    diagonal = up_ref[c // 2, pl.ds(pl.multiple_of(lax.rem(c, 2) * 64, 64), 64), :]
    strip = jnp.where(r // 2 > c // 2, strip, jnp.where(r // 2 == c // 2, diagonal, 0.0))
    odd = lax.rem(r, 2) == 1
    factor_out[...] = jnp.transpose(jnp.where(odd, pltpu.roll(strip, 64, 1), strip))[:64, :]

    inverse = jnp.where(
        lax.broadcasted_iota(jnp.int32, (width, width), 1) // 128
        <= lax.broadcasted_iota(jnp.int32, (width, width), 0) // 128,
        a_ref[...],
        0.0,
    )
    inv = split2(inverse)
    panel_x.finish()
    tile = 256

    def panel_tile(target, source, factor):
        @pl.loop(0, span // tile)
        def _(t):
            lanes = pl.ds(pl.multiple_of(t * tile, tile), tile)
            target[:, lanes] = dot3(factor, split2(source[:, :, lanes].reshape(width, tile)))

    panel_tile(left_x, all_columns, inv)
    lower_out[...] = left_x[pl.ds(pl.multiple_of(c * 64, 64), 64), :]
    pass_on(2)
    parts = [contract(x, chosen, 1, 1) for x in split3(inverse)]
    inv_pivot = split2(parts[0] + parts[1] + parts[2])
    for d in range(2):
        panel_z(far - 1, d).wait_recv()
    panel_tile(right_x, all_rows, inv_pivot)
    upper_out[...] = right_x[pl.ds(pl.multiple_of(r * 64, 64), 64), :]

    pass_on(3)

    right = split2(right_x[...])

    @pl.loop(0, span // BS)
    def _(t):
        rows = pl.ds(pl.multiple_of(t * BS, BS), BS)
        update[t, :, :] = dot3(split2(jnp.transpose(left_x[:, rows])), right)

    def subtract(k, h, s):
        first, count = SUBS[s]
        into = pl.ds(first - PANEL, count)
        update[k * 2 + h, into, :] = fin[k, h, pl.ds(first, count), :] - update[k * 2 + h, into, :]

    pass_on(4)
    for s in range(1, len(SUBS)):
        for h in range(2):
            subtract(m, h, s)
    for s in range(1, len(SUBS)):
        for d in range(2):
            ring(5, d, s).wait_recv()
        for k in (1, -1):
            for h in range(2):
                subtract(layer(k), h, s)
    for s in range(1, len(SUBS)):
        for d in range(2):
            ring(6, d, s).wait_recv()
        for h in range(2):
            subtract(layer(2), h, s)

    for s in range(len(SUBS)):
        for t in range(1, 7):
            for d in range(2):
                ring(t, d, s).wait_send()
    for k in range(1, LAYERS):
        diag_y(k).wait_send()
    for i in range(len(stages)):
        stage_z(i, "send")
    diag_x.drain()
    panel_x.drain()
    for j in range(far):
        for d in range(2):
            panel_z(j, d).wait_send()


def store_kernel(*refs):
    ins, outs, sem = refs[:4], refs[4:8], refs[8]
    copies = [pltpu.make_async_copy(ins[3].at[i], outs[3].at[i], sem.at[3 + i]) for i in range(ins[3].shape[0])]
    copies += [pltpu.make_async_copy(ins[i], outs[i], sem.at[i]) for i in range(3)]
    for copy in copies:
        copy.start()
    for copy in copies:
        copy.wait()


def per_device(diag_parts, column_parts, row_parts, schur_parts, block_pattern, pivot_order):
    rows_dev, cols_dev = schur_parts.shape[1:]
    width = pivot_order.shape[0]
    grid_rows, grid_cols = lax.axis_size("row"), lax.axis_size("col")
    vmem = pl.BlockSpec(memory_space=pltpu.VMEM)
    anywhere = pl.BlockSpec(memory_space=pl.ANY)
    dma = pltpu.SemaphoreType.DMA
    subs = len(SUBS)
    chips = max(grid_cols // 4, 1)
    shapes = (
        diag_parts.shape[1:],
        column_parts.shape[:0:-1],
        row_parts.shape[1:],
        (rows_dev // BS, BS, cols_dev),
    )
    held = pl.pallas_call(
        functools.partial(kernel, grid_rows, grid_cols),
        out_shape=tuple(pltpu.VMEM(shape, F32) for shape in shapes),
        in_specs=[pl.BlockSpec(memory_space=pltpu.HBM)] * 6,
        out_specs=[vmem] * 4,
        scratch_shapes=[
            pltpu.VMEM(diag_parts.shape[1:], F32),
            pltpu.VMEM(block_pattern.shape[1:], jnp.int32),
            pltpu.VMEM((1, width), jnp.int32),
            pltpu.VMEM((LAYERS, 2, HALF, cols_dev), F32),
            pltpu.VMEM((LAYERS, 2, HALF, cols_dev), F32),
            pltpu.VMEM((2, HALF, cols_dev), F32),
            pltpu.VMEM((2, 2, HALF, cols_dev), F32),
            pltpu.VMEM(column_parts.shape[:0:-1], F32),
            pltpu.VMEM(row_parts.shape[1:], F32),
            pltpu.VMEM((rows_dev // BS, cols_dev), F32),
            pltpu.VMEM((LAYERS, 32, 128), F32),
            pltpu.VMEM((grid_cols, grid_rows, 32, 128), F32),
            pltpu.VMEM((grid_rows, 2, 32, width), F32),
            pltpu.VMEM((grid_cols, 64, rows_dev), F32),
            pltpu.VMEM((grid_rows, 64, cols_dev), F32),
            pltpu.VMEM((width, width), F32),
            pltpu.VMEM((128, 128), F32),
            pltpu.VMEM((width // 128, 128, 128), F32),
            pltpu.VMEM((width, rows_dev), F32),
            pltpu.VMEM((width, cols_dev), F32),
            dma((13,)),
            dma((6, 2, subs)),
            dma((6, 2, subs)),
            dma((LAYERS - 1,)),
            dma((LAYERS - 1,)),
            dma((grid_rows - 1, 2)),
            dma((grid_rows - 1, 2)),
            dma((chips, 2)),
            dma((chips, 2)),
            dma((1 + 2 * chips,)),
            dma((1 + 2 * chips,)),
            dma((grid_rows // 2, 2)),
            dma((grid_rows // 2, 2)),
            dma((chips, 2)),
            dma((chips, 2)),
            dma((1 + 2 * chips,)),
            dma((1 + 2 * chips,)),
        ],
        compiler_params=pltpu.CompilerParams(
            collective_id=0, has_side_effects=True, vmem_limit_bytes=48 << 20
        ),
    )(
        *(
            pltpu.with_memory_space_constraint(x, pltpu.HBM)
            for x in (
                diag_parts[0],
                block_pattern[0],
                pivot_order.reshape(1, width),
                column_parts[0].T,
                row_parts[0],
                schur_parts[0],
            )
        )
    )
    factor, lower_t, upper, schur = pl.pallas_call(
        store_kernel,
        out_shape=tuple(jax.ShapeDtypeStruct(shape, F32) for shape in shapes),
        in_specs=[vmem] * 4,
        out_specs=[anywhere] * 4,
        scratch_shapes=[dma((3 + rows_dev // BS,))],
        compiler_params=pltpu.CompilerParams(vmem_limit_bytes=8 << 20),
    )(*held)
    return factor, lower_t.T, upper, schur.reshape(rows_dev, cols_dev)


def solution(mesh):
    placed = (
        P("gz", "row", "col"),
        P("gz", "row", "col"),
        P("gz", "row", "col"),
        P("gz", "row", "col"),
        P("gz", "row", "col"),
        P(),
    )
    return jax.shard_map(
        per_device,
        mesh=mesh,
        in_specs=placed,
        out_specs=(P("row", "col"), P("row", "col"), P("row", "col"), P("row", "col")),
        check_vma=False,
    )
```

```python
import functools

import jax
import jax.numpy as jnp
from jax import lax
from jax.experimental import pallas as pl
from jax.experimental.pallas import tpu as pltpu
from jax.sharding import PartitionSpec as P

BS = 128
LAYERS = 4
PANEL = 16
HALF = PANEL + BS
SUBS = ((0, 16), (16, 32), (48, 32), (80, 32), (112, 32))
HI = lax.Precision.HIGHEST
F32 = jnp.float32
BF16 = jnp.bfloat16
MESH = pl.DeviceIdType.MESH


def split2(x):
    hi = x.astype(BF16)
    return hi, (x - hi.astype(F32)).astype(BF16)


def split3(x):
    hi = x.astype(BF16)
    rest = x - hi.astype(F32)
    mid = rest.astype(BF16)
    return hi, mid, (rest - mid.astype(F32)).astype(BF16)


def contract(a, b, da, db):
    return lax.dot_general(a, b, (((da,), (db,)), ((), ())), preferred_element_type=F32)


def dot3(a, b):
    return contract(a[0], b[0], 1, 0) + (contract(a[0], b[1], 1, 0) + contract(a[1], b[0], 1, 0))


def eliminate_group(d_ref, q):
    lane = lax.broadcasted_iota(jnp.int32, (8, 128), 1)
    sub = lax.broadcasted_iota(jnp.int32, (8, 128), 0)
    lo = 8 * q
    g = d_ref[lo : lo + 8, :]
    col = [jnp.broadcast_to(g[:, lo + j : lo + j + 1], (8, 128)) for j in range(8)]
    snap = jnp.zeros((8, 128), F32)
    pivots = jnp.ones((8, 128), F32)
    for k in range(8):
        piv = jnp.broadcast_to(col[k][k : k + 1, :], (8, 128))
        f = jnp.where(sub != k, col[k] * (1.0 / piv), 0.0)
        for j in range(k + 1, 8):
            col[j] = col[j] - f * jnp.broadcast_to(col[j][k : k + 1, :], (8, 128))
        g = jnp.where(lane == lo + k, jnp.where(sub == k, 1.0, 0.0), g)
        top = jnp.broadcast_to(g[k : k + 1, :], (8, 128))
        snap = jnp.where(sub == k, top, snap)
        pivots = jnp.where(sub == k, piv, pivots)
        g = g - f * top
    w = g / pivots
    if q < 15:
        below = d_ref[lo + 8 : lo + 16, :]
        acc = jnp.where((lane >= lo) & (lane < lo + 8), 0.0, below)
        for j in range(8):
            acc = acc - jnp.broadcast_to(below[:, lo + j : lo + j + 1], (8, 128)) * jnp.broadcast_to(
                w[j : j + 1, :], (8, 128)
            )
        d_ref[lo + 8 : lo + 16, :] = acc
    if q < 14:
        gh, gm, gl = (x.astype(F32) for x in split3(d_ref[lo : lo + 8, :]))
        wh, wm, wl = (x.astype(F32) for x in split3(w))
        update = contract(
            jnp.concatenate([gh, gh, gm, gh, gm, gl], axis=0).astype(BF16),
            jnp.concatenate([wh, wm, wh, wl, wm, wh], axis=0).astype(BF16),
            0,
            0,
        )
        rest = d_ref[lo + 16 : 128, :]
        lane_r = lax.broadcasted_iota(jnp.int32, rest.shape, 1)
        d_ref[lo + 16 : 128, :] = jnp.where((lane_r >= lo) & (lane_r < lo + 8), 0.0, rest) - update[lo + 16 :, :]
    d_ref[lo : lo + 8, :] = jnp.where(lane == lo + sub, 1.0, snap) * lax.rsqrt(pivots)
    return jnp.sqrt(pivots)


def eliminate_block(a_ref, d_ref, up_ref, i, hook):
    width = a_ref.shape[0]
    at = pl.multiple_of(i * 128, 128)
    rows = pl.ds(at, 128)
    d_ref[...] = a_ref[rows, pl.ds(at, 128)]
    diagonal = []
    for q in range(16):
        if q % 4 == 0:
            hook(i, q // 4)
        diagonal.append(eliminate_group(d_ref, q))
    r = lax.broadcasted_iota(jnp.int32, (128, 128), 0)
    c = lax.broadcasted_iota(jnp.int32, (128, 128), 1)
    d = d_ref[...]
    inverse = jnp.where(c <= r, d, 0.0)
    upper = jnp.where(c > r, d, jnp.where(c == r, jnp.concatenate(diagonal, axis=0), 0.0))
    up_ref[i] = upper
    a_ref[rows, :] = jnp.dot(inverse, a_ref[rows, :], precision=HI, preferred_element_type=F32)
    a_ref[rows, pl.ds(at, 128)] = inverse

    @pl.loop(i + 1, width // 128)
    def _(j):
        below = pl.ds(pl.multiple_of(j * 128, 128), 128)
        a_ref[below, pl.ds(at, 128)] = jnp.zeros((128, 128), F32)
        a_ref[below, :] = a_ref[below, :] - lax.dot_general(
            a_ref[rows, below], a_ref[rows, :], (((0,), (0,)), ((), ())), precision=HI, preferred_element_type=F32
        )


def kernel(
    grid_rows, grid_cols,
    diag_hbm, pattern_hbm, pivot_hbm, column_ref, row_ref, schur_ref,
    factor_out, lower_out, upper_out, update,
    diag_ref, pattern_ref, pivot_ref, w, fin, rs1, rsx, weights,
    layer_diag, grid_diag, full_diag, all_columns, all_rows, a_ref, d_ref, up_ref, left_x, right_x,
    load_sem, y_send, y_recv, dy_send, dy_recv, dz_send, dz_recv, dx_send, dx_recv, dc_send, dc_recv,
    pz_send, pz_recv, px_send, px_recv, pc_send, pc_recv, x_word, beside_in, all_in,
):
    m = lax.axis_index("gz")
    r = lax.axis_index("row")
    c = lax.axis_index("col")
    width = a_ref.shape[0]
    span = fin.shape[3]
    blocks = width // 128

    def layer(k):
        return lax.rem(m + k + LAYERS, LAYERS)

    def row_peer(k):
        return lax.rem(r + k + grid_rows, grid_rows)

    def col_peer(k):
        return lax.rem(c + k + grid_cols, grid_cols)

    other_core = c + 1 - 2 * lax.rem(c, 2)

    def in_line(here, step, count):
        return jnp.logical_and(here + step >= 0, here + step < count)

    barrier = pltpu.get_barrier_semaphore()
    for k in range(1, LAYERS):
        pl.semaphore_signal(barrier, inc=1, device_id=(layer(k), r, c), device_id_type=MESH)
    sides = [(r, 1, grid_rows), (r, -1, grid_rows), (c, 2, grid_cols), (c, -2, grid_cols)]

    def side(i):
        step = sides[i][1]
        place = (m, row_peer(step), c) if i < 2 else (m, r, col_peer(step))
        return place, in_line(*sides[i])

    for i in range(4):
        place, there = side(i)

        @pl.when(jnp.logical_and(there, m == 0))
        def _(place=place):
            pl.semaphore_signal(barrier, inc=1, device_id=place, device_id_type=MESH)

    pl.semaphore_signal(barrier, inc=1, device_id=(m, r, other_core), device_id_type=MESH)

    small = [
        pltpu.make_async_copy(x, y, load_sem.at[16 + i])
        for i, (x, y) in enumerate(((diag_hbm, diag_ref), (pattern_hbm, pattern_ref), (pivot_hbm, pivot_ref)))
    ]

    def load_panel(k, h):
        block = k * 2 + h
        return pltpu.make_async_copy(
            (column_ref, row_ref)[h].at[pl.ds(pl.multiple_of(k * PANEL, PANEL), PANEL), :],
            w.at[k, h, pl.ds(0, PANEL), :],
            load_sem.at[8 + block],
        )

    def load_front(k, h):
        block = k * 2 + h
        return pltpu.make_async_copy(
            schur_ref.at[pl.ds(pl.multiple_of(block * BS, BS), BS), :],
            w.at[k, h, pl.ds(PANEL, BS), :],
            load_sem.at[block],
        )

    order = [(layer(k), h) for k in (2, 1, -1, 0) for h in range(2)]
    small[0].start()
    for k, h in order:
        load_panel(k, h).start()
    for load in small[1:]:
        load.start()
    for k, h in order:
        load_front(k, h).start()

    def ring(t, d, s):
        step = 1 - 2 * d
        to = layer(step)
        first, count = SUBS[s]
        rows = pl.ds(first, count)
        if t == 1:
            src, dst = w.at[layer(2), d, rows], rs1.at[d, rows]
        elif t == 2:
            src, dst = w.at[to, 1 - d, rows], rsx.at[d, 1 - d, rows]
        elif t == 3:
            src, dst = w.at[to, d, rows], rsx.at[d, d, rows]
        elif t == 4:
            src = dst = fin.at[m, d, rows]
        elif t == 5:
            src = dst = fin.at[m, 1 - d, rows]
        else:
            src = dst = fin.at[layer(-step), d, rows]
        return pltpu.make_async_remote_copy(
            src_ref=src, dst_ref=dst, send_sem=y_send.at[t - 1, d, s], recv_sem=y_recv.at[t - 1, d, s],
            device_id=(to, r, c), device_id_type=MESH,
        )

    def add_opposite(s):
        first, count = SUBS[s]
        rows = pl.ds(first, count)
        for d in range(2):
            ring(1, d, s).wait_recv()
            to = layer(1 - 2 * d)
            w[to, d, rows, :] = w[to, d, rows, :] + rs1[d, rows, :]
            ring(3, d, s).start()

    def finish_sum(s):
        first, count = SUBS[s]
        rows = pl.ds(first, count)
        for d in range(2):
            ring(2, d, s).wait_recv()
            ring(3, d, s).wait_recv()
        for h in range(2):
            fin[m, h, rows, :] = w[m, h, rows, :] + rsx[0, h, rows, :] + rsx[1, h, rows, :]
        for t in (4, 5):
            for d in range(2):
                ring(t, d, s).start()

    def pass_on(s):
        for d in range(2):
            ring(4, d, s).wait_recv()
            ring(6, d, s).start()

    def arrived(s):
        for d in range(2):
            ring(5, d, s).wait_recv()
            ring(6, d, s).wait_recv()

    def diag_y(k):
        return pltpu.make_async_remote_copy(
            src_ref=layer_diag.at[m], dst_ref=layer_diag.at[m], send_sem=dy_send.at[k - 1], recv_sem=dy_recv.at[k - 1],
            device_id=(layer(k), r, c), device_id_type=MESH,
        )

    stages = [[k for k in stage if k < grid_rows] for stage in ((1,), (2,), (3, 4), (5, 6, 7))]

    def along_z(k, act):
        for d in range(2):
            to = r + k * (1 - 2 * d)
            copy = pltpu.make_async_remote_copy(
                src_ref=grid_diag.at[c, r], dst_ref=grid_diag.at[c, r],
                send_sem=dz_send.at[k - 1, d], recv_sem=dz_recv.at[k - 1, d],
                device_id=(m, lax.rem(to + grid_rows, grid_rows), c), device_id_type=MESH,
            )
            ahead, behind = to < grid_rows, to >= 0
            if act == "recv":
                ahead, behind = r - k * (1 - 2 * d) < grid_rows, r - k * (1 - 2 * d) >= 0

            @pl.when(jnp.logical_and(ahead, behind))
            def _(copy=copy):
                if act == "start":
                    copy.start()
                elif act == "recv":
                    copy.wait_recv()
                else:
                    copy.wait_send()

    def stage_z(i, act):
        for k in stages[i]:
            along_z(k, act)

    class AlongX:
        def __init__(self, ref, sems):
            self.ref, self.sems, self.steps = ref, sems, grid_cols // 4

        def part(self, j, d):
            block = col_peer(2 * j * (2 * d - 1))
            if j == self.steps - 1:
                half = self.ref.shape[1] // 2
                return self.ref.at[block, pl.ds(half * d, half)]
            return self.ref.at[block]

        def chip(self, j, d):
            ref = self.part(j, d)
            return pltpu.make_async_remote_copy(
                src_ref=ref, dst_ref=ref, send_sem=self.sems[0].at[j, d], recv_sem=self.sems[1].at[j, d],
                device_id=(m, r, col_peer(2 - 4 * d)), device_id_type=MESH,
            )

        def core(self, i):
            if i == 0:
                ref = self.ref.at[c]
            else:
                j, d = divmod(i - 1, 2)
                block = col_peer(2 * (j + 1) * (2 * d - 1))
                ref = self.ref.at[block]
                if j == self.steps - 1:
                    half = self.ref.shape[1] // 2
                    ref = self.ref.at[block, pl.ds(half * d, half)]
            return pltpu.make_async_remote_copy(
                src_ref=ref, dst_ref=ref, send_sem=self.sems[2].at[i], recv_sem=self.sems[3].at[i],
                device_id=(m, r, other_core), device_id_type=MESH,
            )

        def start(self):
            for d in range(2):
                if self.steps:
                    self.chip(0, d).start()
            self.core(0).start()

        def go_on(self, j):
            for d in range(2):
                self.chip(j, d).wait_recv()
                if j + 1 < self.steps:
                    self.chip(j + 1, d).start()
                self.core(1 + 2 * j + d).start()

        def finish(self):
            for i in range(1 + 2 * self.steps):
                self.core(i).wait_recv()

        def drain(self):
            for i in range(1 + 2 * self.steps):
                self.core(i).wait_send()
            for j in range(self.steps):
                for d in range(2):
                    self.chip(j, d).wait_send()

    diag_x = AlongX(grid_diag, (dx_send, dx_recv, dc_send, dc_recv))
    panel_x = AlongX(all_columns, (px_send, px_recv, pc_send, pc_recv))

    def send(t, s):
        for d in range(2):
            ring(t, d, s).start()

    def mask_front(k, h):
        load_front(k, h).wait()
        w[k, h, PANEL:HALF, :] = w[k, h, PANEL:HALF, :] * weights[pl.ds(k * 2 + h, 1), :]

    words = max(grid_cols // 2 - 2, 0)

    def word(i, act):
        for d in range(2):
            step = 2 - 4 * d
            @pl.when(in_line(c, step if act == "send" else -step, grid_cols))
            def _(d=d, step=step):
                if act == "send":
                    pl.semaphore_signal(
                        x_word.at[i, d], inc=1, device_id=(m, r, col_peer(step)), device_id_type=MESH
                    )
                else:
                    pl.semaphore_wait(x_word.at[i, d], 1)

    small[0].wait()
    layer_diag[m] = jnp.concatenate([diag_ref[:32, :], diag_ref[32:, :]], axis=1)
    beside = sum(in_line(*at).astype(jnp.int32) for at in sides)
    pl.semaphore_wait(barrier, LAYERS - 1 + 1 + jnp.where(m == 0, beside, 0))

    def layers_in():
        for i in range(4):
            place, there = side(i)

            @pl.when(jnp.logical_and(there, m == 0))
            def _(i=i, place=place):
                pl.semaphore_signal(beside_in.at[i ^ 1], inc=1, device_id=place, device_id_type=MESH)

    def sides_in():
        for i in range(4):
            _, there = side(i)

            @pl.when(jnp.logical_and(there, m == 0))
            def _(i=i):
                pl.semaphore_wait(beside_in.at[i], 1)

        @pl.when(m == 0)
        def _():
            for k in range(1, LAYERS):
                pl.semaphore_signal(all_in, inc=1, device_id=(layer(k), r, c), device_id_type=MESH)

        @pl.when(m != 0)
        def _():
            pl.semaphore_wait(all_in, 1)

    layers_in()
    for k in range(1, LAYERS):
        diag_y(k).start()
    for k, h in order[:6]:
        load_panel(k, h).wait()
    send(1, 0)
    send(2, 0)
    for load in small[1:]:
        load.wait()
    pattern = pattern_ref[...].astype(F32)
    weights[...] = jnp.concatenate(
        [jnp.broadcast_to(pattern[:, j : j + 1], (pattern.shape[0], BS)) for j in range(pattern.shape[1])], axis=1
    )
    for k, h in order[:2]:
        mask_front(k, h)
    send(1, 1)
    for k in range(1, LAYERS):
        diag_y(k).wait_recv()
    grid_diag[c, r] = layer_diag[0] + layer_diag[1] + layer_diag[2] + layer_diag[3]
    sides_in()
    stage_z(0, "start")
    if words:
        word(0, "send")
    add_opposite(0)
    send(1, 2)
    for i in range(words):
        word(i, "wait")
        if i + 1 < words:
            word(i + 1, "send")
    for k, h in order[2:6]:
        mask_front(k, h)
    stage_z(0, "recv")
    stage_z(1, "start")
    for k, h in order[6:]:
        load_panel(k, h).wait()
    finish_sum(0)
    send(1, 3)
    stage_z(1, "recv")
    stage_z(2, "start")
    pass_on(0)
    send(1, 4)
    for s in range(1, len(SUBS)):
        send(2, s)
    for k, h in order[6:]:
        mask_front(k, h)
    stage_z(2, "recv")
    stage_z(3, "start")
    stage_z(3, "recv")
    diag_x.start()

    far = grid_rows // 2

    def panel_z(j, d):
        step = 1 - 2 * d
        block = row_peer(-step * j)
        ref = all_rows.at[block, pl.ds(32 * d, 32)] if j == far - 1 else all_rows.at[block]
        return pltpu.make_async_remote_copy(
            src_ref=ref, dst_ref=ref, send_sem=pz_send.at[j, d], recv_sem=pz_recv.at[j, d],
            device_id=(m, row_peer(step), c), device_id_type=MESH,
        )

    def spread_panels(s):
        arrived(s)
        for k in range(LAYERS):
            all_columns[c, k * PANEL : (k + 1) * PANEL, :] = fin[k, 0, 0:PANEL, :]
            all_rows[r, k * PANEL : (k + 1) * PANEL, :] = fin[k, 1, 0:PANEL, :]
        for d in range(2):
            panel_z(0, d).start()
        panel_x.start()

    def rows_on(j):
        for d in range(2):
            panel_z(j - 1, d).wait_recv()
            panel_z(j, d).start()

    def columns_on(j):
        panel_x.go_on(j)

    add_opposite(1)
    add_opposite(2)
    for j in range(diag_x.steps):
        diag_x.go_on(j)
    spread_panels(0)
    add_opposite(3)
    add_opposite(4)
    diag_x.finish()

    low = lax.broadcasted_iota(jnp.int32, (grid_rows, 32, 128), 2) < 64
    for pair in range(grid_cols // 2):
        left, right = grid_diag[2 * pair], grid_diag[2 * pair + 1]
        lanes = slice(pair * 128, (pair + 1) * 128)
        full_diag[:, 0, :, lanes] = jnp.where(low, left, pltpu.roll(right, 64, 2))
        full_diag[:, 1, :, lanes] = jnp.where(low, pltpu.roll(left, 64, 2), right)
    chosen = (lax.broadcasted_iota(jnp.int32, (width, width), 0) == pivot_ref[...]).astype(BF16)
    full = full_diag[...].reshape(width, width)
    parts = [contract(chosen, x, 0, 0) for x in split3(full)]
    a_ref[...] = parts[0] + parts[1] + parts[2]

    slots = {
        (0, 0): [(finish_sum, 1)],
        (0, 1): [(rows_on, 1), (columns_on, 0)],
        (0, 3): [(finish_sum, 2)],
        (1, 1): [(finish_sum, 3), (columns_on, 1)],
        (1, 3): [(rows_on, 2)],
        (2, 0): [(finish_sum, 4)],
        (2, 3): [(rows_on, 3)],
        (3, 2): [(pass_on, 1)],
    }
    slots = {at: [
            (f, s) for f, s in work if not (f is rows_on and s >= far) and not (f is columns_on and s >= panel_x.steps)
        ]
        for at, work in slots.items()}

    def hook(i, at):
        for (block, place), work in slots.items():
            if place == at and block < blocks and work:
                @pl.when(i == block)
                def _(work=work):
                    for f, s in work:
                        f(s)

    def hooks_after(least, most):
        for (block, place), work in sorted(slots.items()):
            if least <= block <= most:
                for f, s in work:
                    f(s)

    @pl.loop(0, blocks)
    def _(i):
        eliminate_block(a_ref, d_ref, up_ref, i, hook)

    hooks_after(blocks, 4)

    strip = a_ref[pl.ds(pl.multiple_of(c * 64, 64), 64), pl.ds(pl.multiple_of((r // 2) * 128, 128), 128)]
    diagonal = up_ref[c // 2, pl.ds(pl.multiple_of(lax.rem(c, 2) * 64, 64), 64), :]
    strip = jnp.where(r // 2 > c // 2, strip, jnp.where(r // 2 == c // 2, diagonal, 0.0))
    odd = lax.rem(r, 2) == 1
    factor_out[...] = jnp.transpose(jnp.where(odd, pltpu.roll(strip, 64, 1), strip))[:64, :]

    inverse = jnp.where(
        lax.broadcasted_iota(jnp.int32, (width, width), 1) // 128
        <= lax.broadcasted_iota(jnp.int32, (width, width), 0) // 128,
        a_ref[...],
        0.0,
    )
    inv = split2(inverse)
    panel_x.finish()
    tile = 256

    def panel_tile(target, source, factor):
        @pl.loop(0, span // tile)
        def _(t):
            lanes = pl.ds(pl.multiple_of(t * tile, tile), tile)
            target[:, lanes] = dot3(factor, split2(source[:, :, lanes].reshape(width, tile)))

    panel_tile(left_x, all_columns, inv)
    lower_out[...] = left_x[pl.ds(pl.multiple_of(c * 64, 64), 64), :]
    pass_on(2)
    parts = [contract(x, chosen, 1, 1) for x in split3(inverse)]
    inv_pivot = split2(parts[0] + parts[1] + parts[2])
    for d in range(2):
        panel_z(far - 1, d).wait_recv()
    panel_tile(right_x, all_rows, inv_pivot)
    upper_out[...] = right_x[pl.ds(pl.multiple_of(r * 64, 64), 64), :]

    pass_on(3)

    right = split2(right_x[...])

    @pl.loop(0, span // BS)
    def _(t):
        rows = pl.ds(pl.multiple_of(t * BS, BS), BS)
        update[t, :, :] = dot3(split2(jnp.transpose(left_x[:, rows])), right)

    def subtract(k, h, s):
        first, count = SUBS[s]
        into = pl.ds(first - PANEL, count)
        update[k * 2 + h, into, :] = fin[k, h, pl.ds(first, count), :] - update[k * 2 + h, into, :]

    pass_on(4)
    for s in range(1, len(SUBS)):
        for h in range(2):
            subtract(m, h, s)
    for s in range(1, len(SUBS)):
        for d in range(2):
            ring(5, d, s).wait_recv()
        for k in (1, -1):
            for h in range(2):
                subtract(layer(k), h, s)
    for s in range(1, len(SUBS)):
        for d in range(2):
            ring(6, d, s).wait_recv()
        for h in range(2):
            subtract(layer(2), h, s)

    for s in range(len(SUBS)):
        for t in range(1, 7):
            for d in range(2):
                ring(t, d, s).wait_send()
    for k in range(1, LAYERS):
        diag_y(k).wait_send()
    for i in range(len(stages)):
        stage_z(i, "send")
    diag_x.drain()
    panel_x.drain()
    for j in range(far):
        for d in range(2):
            panel_z(j, d).wait_send()


def store_kernel(*refs):
    ins, outs, sem = refs[:4], refs[4:8], refs[8]
    copies = [pltpu.make_async_copy(ins[3].at[i], outs[3].at[i], sem.at[3 + i]) for i in range(ins[3].shape[0])]
    copies += [pltpu.make_async_copy(ins[i], outs[i], sem.at[i]) for i in range(3)]
    for copy in copies:
        copy.start()
    for copy in copies:
        copy.wait()


def per_device(diag_parts, column_parts, row_parts, schur_parts, block_pattern, pivot_order):
    rows_dev, cols_dev = schur_parts.shape[1:]
    width = pivot_order.shape[0]
    grid_rows, grid_cols = lax.axis_size("row"), lax.axis_size("col")
    vmem = pl.BlockSpec(memory_space=pltpu.VMEM)
    anywhere = pl.BlockSpec(memory_space=pl.ANY)
    dma = pltpu.SemaphoreType.DMA
    subs = len(SUBS)
    chips = max(grid_cols // 4, 1)
    shapes = (
        diag_parts.shape[1:],
        column_parts.shape[:0:-1],
        row_parts.shape[1:],
        (rows_dev // BS, BS, cols_dev),
    )
    held = pl.pallas_call(
        functools.partial(kernel, grid_rows, grid_cols),
        out_shape=tuple(pltpu.VMEM(shape, F32) for shape in shapes),
        in_specs=[pl.BlockSpec(memory_space=pltpu.HBM)] * 6,
        out_specs=[vmem] * 4,
        scratch_shapes=[
            pltpu.VMEM(diag_parts.shape[1:], F32),
            pltpu.VMEM(block_pattern.shape[1:], jnp.int32),
            pltpu.VMEM((1, width), jnp.int32),
            pltpu.VMEM((LAYERS, 2, HALF, cols_dev), F32),
            pltpu.VMEM((LAYERS, 2, HALF, cols_dev), F32),
            pltpu.VMEM((2, HALF, cols_dev), F32),
            pltpu.VMEM((2, 2, HALF, cols_dev), F32),
            pltpu.VMEM((rows_dev // BS, cols_dev), F32),
            pltpu.VMEM((LAYERS, 32, 128), F32),
            pltpu.VMEM((grid_cols, grid_rows, 32, 128), F32),
            pltpu.VMEM((grid_rows, 2, 32, width), F32),
            pltpu.VMEM((grid_cols, 64, rows_dev), F32),
            pltpu.VMEM((grid_rows, 64, cols_dev), F32),
            pltpu.VMEM((width, width), F32),
            pltpu.VMEM((128, 128), F32),
            pltpu.VMEM((width // 128, 128, 128), F32),
            pltpu.VMEM((width, rows_dev), F32),
            pltpu.VMEM((width, cols_dev), F32),
            dma((19,)),
            dma((6, 2, subs)),
            dma((6, 2, subs)),
            dma((LAYERS - 1,)),
            dma((LAYERS - 1,)),
            dma((grid_rows - 1, 2)),
            dma((grid_rows - 1, 2)),
            dma((chips, 2)),
            dma((chips, 2)),
            dma((1 + 2 * chips,)),
            dma((1 + 2 * chips,)),
            dma((grid_rows // 2, 2)),
            dma((grid_rows // 2, 2)),
            dma((chips, 2)),
            dma((chips, 2)),
            dma((1 + 2 * chips,)),
            dma((1 + 2 * chips,)),
            pltpu.SemaphoreType.REGULAR((2, 2)),
            pltpu.SemaphoreType.REGULAR((4,)),
            pltpu.SemaphoreType.REGULAR,
        ],
        compiler_params=pltpu.CompilerParams(
            collective_id=0, has_side_effects=True, vmem_limit_bytes=48 << 20
        ),
    )(
        *(
            pltpu.with_memory_space_constraint(x, pltpu.HBM)
            for x in (
                diag_parts[0],
                block_pattern[0],
                pivot_order.reshape(1, width),
                column_parts[0].T,
                row_parts[0],
                schur_parts[0],
            )
        )
    )
    factor, lower_t, upper, schur = pl.pallas_call(
        store_kernel,
        out_shape=tuple(jax.ShapeDtypeStruct(shape, F32) for shape in shapes),
        in_specs=[vmem] * 4,
        out_specs=[anywhere] * 4,
        scratch_shapes=[dma((3 + rows_dev // BS,))],
        compiler_params=pltpu.CompilerParams(vmem_limit_bytes=8 << 20),
    )(*held)
    return factor, lower_t.T, upper, schur.reshape(rows_dev, cols_dev)


def solution(mesh):
    placed = (
        P("gz", "row", "col"),
        P("gz", "row", "col"),
        P("gz", "row", "col"),
        P("gz", "row", "col"),
        P("gz", "row", "col"),
        P(),
    )
    return jax.shard_map(
        per_device,
        mesh=mesh,
        in_specs=placed,
        out_specs=(P("row", "col"), P("row", "col"), P("row", "col"), P("row", "col")),
        check_vma=False,
    )
```

```python
import functools

import jax
import jax.numpy as jnp
from jax import lax
from jax.experimental import pallas as pl
from jax.experimental.pallas import tpu as pltpu
from jax.sharding import PartitionSpec as P

BS = 128
LAYERS = 4
PANEL = 16
HALF = PANEL + BS
SUBS = ((0, 16), (16, 64), (80, 64))
HI = lax.Precision.HIGHEST
F32 = jnp.float32
BF16 = jnp.bfloat16
MESH = pl.DeviceIdType.MESH


def split2(x):
    hi = x.astype(BF16)
    return hi, (x - hi.astype(F32)).astype(BF16)


def split3(x):
    hi = x.astype(BF16)
    rest = x - hi.astype(F32)
    mid = rest.astype(BF16)
    return hi, mid, (rest - mid.astype(F32)).astype(BF16)


def contract(a, b, da, db):
    return lax.dot_general(a, b, (((da,), (db,)), ((), ())), preferred_element_type=F32)


def dot3(a, b):
    return contract(a[0], b[0], 1, 0) + (contract(a[0], b[1], 1, 0) + contract(a[1], b[0], 1, 0))


def eliminate_group(d_ref, q):
    lane = lax.broadcasted_iota(jnp.int32, (8, 128), 1)
    sub = lax.broadcasted_iota(jnp.int32, (8, 128), 0)
    lo = 8 * q
    g = d_ref[lo : lo + 8, :]
    col = [jnp.broadcast_to(g[:, lo + j : lo + j + 1], (8, 128)) for j in range(8)]
    snap = jnp.zeros((8, 128), F32)
    pivots = jnp.ones((8, 128), F32)
    for k in range(8):
        piv = jnp.broadcast_to(col[k][k : k + 1, :], (8, 128))
        f = jnp.where(sub != k, col[k] * (1.0 / piv), 0.0)
        for j in range(k + 1, 8):
            col[j] = col[j] - f * jnp.broadcast_to(col[j][k : k + 1, :], (8, 128))
        g = jnp.where(lane == lo + k, jnp.where(sub == k, 1.0, 0.0), g)
        top = jnp.broadcast_to(g[k : k + 1, :], (8, 128))
        snap = jnp.where(sub == k, top, snap)
        pivots = jnp.where(sub == k, piv, pivots)
        g = g - f * top
    w = g / pivots
    if q < 15:
        below = d_ref[lo + 8 : lo + 16, :]
        acc = jnp.where((lane >= lo) & (lane < lo + 8), 0.0, below)
        for j in range(8):
            acc = acc - jnp.broadcast_to(below[:, lo + j : lo + j + 1], (8, 128)) * jnp.broadcast_to(
                w[j : j + 1, :], (8, 128)
            )
        d_ref[lo + 8 : lo + 16, :] = acc
    if q < 14:
        gh, gm, gl = (x.astype(F32) for x in split3(d_ref[lo : lo + 8, :]))
        wh, wm, wl = (x.astype(F32) for x in split3(w))
        update = contract(
            jnp.concatenate([gh, gh, gm, gh, gm, gl], axis=0).astype(BF16),
            jnp.concatenate([wh, wm, wh, wl, wm, wh], axis=0).astype(BF16),
            0,
            0,
        )
        rest = d_ref[lo + 16 : 128, :]
        lane_r = lax.broadcasted_iota(jnp.int32, rest.shape, 1)
        d_ref[lo + 16 : 128, :] = jnp.where((lane_r >= lo) & (lane_r < lo + 8), 0.0, rest) - update[lo + 16 :, :]
    d_ref[lo : lo + 8, :] = jnp.where(lane == lo + sub, 1.0, snap) * lax.rsqrt(pivots)
    return jnp.sqrt(pivots)


def eliminate_block(a_ref, d_ref, up_ref, i, hook):
    width = a_ref.shape[0]
    at = pl.multiple_of(i * 128, 128)
    rows = pl.ds(at, 128)
    d_ref[...] = a_ref[rows, pl.ds(at, 128)]
    diagonal = []
    for q in range(16):
        if q % 4 == 0:
            hook(i, q // 4)
        diagonal.append(eliminate_group(d_ref, q))
    r = lax.broadcasted_iota(jnp.int32, (128, 128), 0)
    c = lax.broadcasted_iota(jnp.int32, (128, 128), 1)
    d = d_ref[...]
    inverse = jnp.where(c <= r, d, 0.0)
    upper = jnp.where(c > r, d, jnp.where(c == r, jnp.concatenate(diagonal, axis=0), 0.0))
    up_ref[i] = upper
    a_ref[rows, :] = jnp.dot(inverse, a_ref[rows, :], precision=HI, preferred_element_type=F32)
    a_ref[rows, pl.ds(at, 128)] = inverse

    @pl.loop(i + 1, width // 128)
    def _(j):
        below = pl.ds(pl.multiple_of(j * 128, 128), 128)
        a_ref[below, pl.ds(at, 128)] = jnp.zeros((128, 128), F32)
        a_ref[below, :] = a_ref[below, :] - lax.dot_general(
            a_ref[rows, below], a_ref[rows, :], (((0,), (0,)), ((), ())), precision=HI, preferred_element_type=F32
        )


def kernel(
    grid_rows, grid_cols,
    diag_hbm, pattern_hbm, pivot_hbm, column_ref, row_ref, schur_ref,
    factor_out, lower_out, upper_out, update,
    diag_ref, pattern_ref, pivot_ref, w, fin, rs1, rsx, weights,
    layer_diag, grid_diag, full_diag, all_columns, all_rows, a_ref, d_ref, up_ref, left_x, right_x,
    load_sem, y_send, y_recv, dy_send, dy_recv, dz_send, dz_recv, dx_send, dx_recv, dc_send, dc_recv,
    pz_send, pz_recv, px_send, px_recv, pc_send, pc_recv, x_word, beside_in, all_in,
):
    m = lax.axis_index("gz")
    r = lax.axis_index("row")
    c = lax.axis_index("col")
    width = a_ref.shape[0]
    span = fin.shape[3]
    blocks = width // 128

    def layer(k):
        return lax.rem(m + k + LAYERS, LAYERS)

    def row_peer(k):
        return lax.rem(r + k + grid_rows, grid_rows)

    def col_peer(k):
        return lax.rem(c + k + grid_cols, grid_cols)

    other_core = c + 1 - 2 * lax.rem(c, 2)

    def in_line(here, step, count):
        return jnp.logical_and(here + step >= 0, here + step < count)

    barrier = pltpu.get_barrier_semaphore()
    for k in range(1, LAYERS):
        pl.semaphore_signal(barrier, inc=1, device_id=(layer(k), r, c), device_id_type=MESH)
    sides = [(r, 1, grid_rows), (r, -1, grid_rows), (c, 2, grid_cols), (c, -2, grid_cols)]

    def side(i):
        step = sides[i][1]
        place = (m, row_peer(step), c) if i < 2 else (m, r, col_peer(step))
        return place, in_line(*sides[i])

    for i in range(4):
        place, there = side(i)

        @pl.when(jnp.logical_and(there, m == 0))
        def _(place=place):
            pl.semaphore_signal(barrier, inc=1, device_id=place, device_id_type=MESH)

    pl.semaphore_signal(barrier, inc=1, device_id=(m, r, other_core), device_id_type=MESH)

    small = [
        pltpu.make_async_copy(x, y, load_sem.at[16 + i])
        for i, (x, y) in enumerate(((diag_hbm, diag_ref), (pattern_hbm, pattern_ref), (pivot_hbm, pivot_ref)))
    ]

    def load_panel(k, h):
        block = k * 2 + h
        return pltpu.make_async_copy(
            (column_ref, row_ref)[h].at[pl.ds(pl.multiple_of(k * PANEL, PANEL), PANEL), :],
            w.at[k, h, pl.ds(0, PANEL), :],
            load_sem.at[8 + block],
        )

    def load_front(k, h):
        block = k * 2 + h
        return pltpu.make_async_copy(
            schur_ref.at[pl.ds(pl.multiple_of(block * BS, BS), BS), :],
            w.at[k, h, pl.ds(PANEL, BS), :],
            load_sem.at[block],
        )

    order = [(layer(k), h) for k in (2, 1, -1, 0) for h in range(2)]
    small[0].start()
    for k, h in order:
        load_panel(k, h).start()
    for load in small[1:]:
        load.start()
    for k, h in order:
        load_front(k, h).start()

    def ring(t, d, s):
        step = 1 - 2 * d
        to = layer(step)
        first, count = SUBS[s]
        rows = pl.ds(first, count)
        if t == 1:
            src, dst = w.at[layer(2), d, rows], rs1.at[d, rows]
        elif t == 2:
            src, dst = w.at[to, 1 - d, rows], rsx.at[d, 1 - d, rows]
        elif t == 3:
            src, dst = w.at[to, d, rows], rsx.at[d, d, rows]
        elif t == 4:
            src = dst = fin.at[m, d, rows]
        elif t == 5:
            src = dst = fin.at[m, 1 - d, rows]
        else:
            src = dst = fin.at[layer(-step), d, rows]
        return pltpu.make_async_remote_copy(
            src_ref=src, dst_ref=dst, send_sem=y_send.at[t - 1, d, s], recv_sem=y_recv.at[t - 1, d, s],
            device_id=(to, r, c), device_id_type=MESH,
        )

    def add_opposite(s):
        first, count = SUBS[s]
        rows = pl.ds(first, count)
        for d in range(2):
            ring(1, d, s).wait_recv()
            to = layer(1 - 2 * d)
            w[to, d, rows, :] = w[to, d, rows, :] + rs1[d, rows, :]
            ring(3, d, s).start()

    def finish_sum(s):
        first, count = SUBS[s]
        rows = pl.ds(first, count)
        for d in range(2):
            ring(2, d, s).wait_recv()
            ring(3, d, s).wait_recv()
        for h in range(2):
            fin[m, h, rows, :] = w[m, h, rows, :] + rsx[0, h, rows, :] + rsx[1, h, rows, :]
        for t in (4, 5):
            for d in range(2):
                ring(t, d, s).start()

    def pass_on(s):
        for d in range(2):
            ring(4, d, s).wait_recv()
            ring(6, d, s).start()

    def arrived(s):
        for d in range(2):
            ring(5, d, s).wait_recv()
            ring(6, d, s).wait_recv()

    def diag_y(k):
        return pltpu.make_async_remote_copy(
            src_ref=layer_diag.at[m], dst_ref=layer_diag.at[m], send_sem=dy_send.at[k - 1], recv_sem=dy_recv.at[k - 1],
            device_id=(layer(k), r, c), device_id_type=MESH,
        )

    stages = [[k for k in stage if k < grid_rows] for stage in ((1,), (2,), (3, 4), (5, 6, 7))]

    def along_z(k, act):
        for d in range(2):
            to = r + k * (1 - 2 * d)
            copy = pltpu.make_async_remote_copy(
                src_ref=grid_diag.at[c, r], dst_ref=grid_diag.at[c, r],
                send_sem=dz_send.at[k - 1, d], recv_sem=dz_recv.at[k - 1, d],
                device_id=(m, lax.rem(to + grid_rows, grid_rows), c), device_id_type=MESH,
            )
            ahead, behind = to < grid_rows, to >= 0
            if act == "recv":
                ahead, behind = r - k * (1 - 2 * d) < grid_rows, r - k * (1 - 2 * d) >= 0

            @pl.when(jnp.logical_and(ahead, behind))
            def _(copy=copy):
                if act == "start":
                    copy.start()
                elif act == "recv":
                    copy.wait_recv()
                else:
                    copy.wait_send()

    def stage_z(i, act):
        for k in stages[i]:
            along_z(k, act)

    class AlongX:
        def __init__(self, ref, sems):
            self.ref, self.sems, self.steps = ref, sems, grid_cols // 4

        def part(self, j, d):
            block = col_peer(2 * j * (2 * d - 1))
            if j == self.steps - 1:
                half = self.ref.shape[1] // 2
                return self.ref.at[block, pl.ds(half * d, half)]
            return self.ref.at[block]

        def chip(self, j, d):
            ref = self.part(j, d)
            return pltpu.make_async_remote_copy(
                src_ref=ref, dst_ref=ref, send_sem=self.sems[0].at[j, d], recv_sem=self.sems[1].at[j, d],
                device_id=(m, r, col_peer(2 - 4 * d)), device_id_type=MESH,
            )

        def core(self, i):
            if i == 0:
                ref = self.ref.at[c]
            else:
                j, d = divmod(i - 1, 2)
                block = col_peer(2 * (j + 1) * (2 * d - 1))
                ref = self.ref.at[block]
                if j == self.steps - 1:
                    half = self.ref.shape[1] // 2
                    ref = self.ref.at[block, pl.ds(half * d, half)]
            return pltpu.make_async_remote_copy(
                src_ref=ref, dst_ref=ref, send_sem=self.sems[2].at[i], recv_sem=self.sems[3].at[i],
                device_id=(m, r, other_core), device_id_type=MESH,
            )

        def start(self):
            for d in range(2):
                if self.steps:
                    self.chip(0, d).start()
            self.core(0).start()

        def go_on(self, j):
            for d in range(2):
                self.chip(j, d).wait_recv()
                if j + 1 < self.steps:
                    self.chip(j + 1, d).start()
                self.core(1 + 2 * j + d).start()

        def finish(self):
            for i in range(1 + 2 * self.steps):
                self.core(i).wait_recv()

        def drain(self):
            for i in range(1 + 2 * self.steps):
                self.core(i).wait_send()
            for j in range(self.steps):
                for d in range(2):
                    self.chip(j, d).wait_send()

    diag_x = AlongX(grid_diag, (dx_send, dx_recv, dc_send, dc_recv))
    panel_x = AlongX(all_columns, (px_send, px_recv, pc_send, pc_recv))

    def send(t, s):
        for d in range(2):
            ring(t, d, s).start()

    def mask_front(k, h):
        load_front(k, h).wait()
        w[k, h, PANEL:HALF, :] = w[k, h, PANEL:HALF, :] * weights[pl.ds(k * 2 + h, 1), :]

    words = max(grid_cols // 2 - 2, 0)

    def word(i, act):
        for d in range(2):
            step = 2 - 4 * d
            @pl.when(in_line(c, step if act == "send" else -step, grid_cols))
            def _(d=d, step=step):
                if act == "send":
                    pl.semaphore_signal(
                        x_word.at[i, d], inc=1, device_id=(m, r, col_peer(step)), device_id_type=MESH
                    )
                else:
                    pl.semaphore_wait(x_word.at[i, d], 1)

    small[0].wait()
    layer_diag[m] = jnp.concatenate([diag_ref[:32, :], diag_ref[32:, :]], axis=1)
    beside = sum(in_line(*at).astype(jnp.int32) for at in sides)
    pl.semaphore_wait(barrier, LAYERS - 1 + 1 + jnp.where(m == 0, beside, 0))

    def layers_in():
        for i in range(4):
            place, there = side(i)

            @pl.when(jnp.logical_and(there, m == 0))
            def _(i=i, place=place):
                pl.semaphore_signal(beside_in.at[i ^ 1], inc=1, device_id=place, device_id_type=MESH)

    def sides_in():
        for i in range(4):
            _, there = side(i)

            @pl.when(jnp.logical_and(there, m == 0))
            def _(i=i):
                pl.semaphore_wait(beside_in.at[i], 1)

        @pl.when(m == 0)
        def _():
            for k in range(1, LAYERS):
                pl.semaphore_signal(all_in, inc=1, device_id=(layer(k), r, c), device_id_type=MESH)

        @pl.when(m != 0)
        def _():
            pl.semaphore_wait(all_in, 1)

    layers_in()
    for k in range(1, LAYERS):
        diag_y(k).start()
    for k, h in order[:6]:
        load_panel(k, h).wait()
    send(1, 0)
    send(2, 0)
    for load in small[1:]:
        load.wait()
    pattern = pattern_ref[...].astype(F32)
    weights[...] = jnp.concatenate(
        [jnp.broadcast_to(pattern[:, j : j + 1], (pattern.shape[0], BS)) for j in range(pattern.shape[1])], axis=1
    )
    for k, h in order[:2]:
        mask_front(k, h)
    send(1, 1)
    for k in range(1, LAYERS):
        diag_y(k).wait_recv()
    grid_diag[c, r] = layer_diag[0] + layer_diag[1] + layer_diag[2] + layer_diag[3]
    sides_in()
    stage_z(0, "start")
    if words:
        word(0, "send")
    add_opposite(0)
    send(1, 2)
    for i in range(words):
        word(i, "wait")
        if i + 1 < words:
            word(i + 1, "send")
    for k, h in order[2:6]:
        mask_front(k, h)
    stage_z(0, "recv")
    stage_z(1, "start")
    for k, h in order[6:]:
        load_panel(k, h).wait()
        mask_front(k, h)
    stage_z(1, "recv")
    stage_z(2, "start")
    finish_sum(0)
    send(2, 1)
    stage_z(2, "recv")
    stage_z(3, "start")
    pass_on(0)
    send(2, 2)
    stage_z(3, "recv")
    diag_x.start()

    far = grid_rows // 2

    def panel_z(j, d):
        step = 1 - 2 * d
        block = row_peer(-step * j)
        ref = all_rows.at[block, pl.ds(32 * d, 32)] if j == far - 1 else all_rows.at[block]
        return pltpu.make_async_remote_copy(
            src_ref=ref, dst_ref=ref, send_sem=pz_send.at[j, d], recv_sem=pz_recv.at[j, d],
            device_id=(m, row_peer(step), c), device_id_type=MESH,
        )

    def spread_panels(s):
        arrived(s)
        for k in range(LAYERS):
            all_columns[c, k * PANEL : (k + 1) * PANEL, :] = fin[k, 0, 0:PANEL, :]
            all_rows[r, k * PANEL : (k + 1) * PANEL, :] = fin[k, 1, 0:PANEL, :]
        for d in range(2):
            panel_z(0, d).start()
        panel_x.start()

    def rows_on(j):
        for d in range(2):
            panel_z(j - 1, d).wait_recv()
            panel_z(j, d).start()

    def columns_on(j):
        panel_x.go_on(j)

    add_opposite(1)
    for j in range(diag_x.steps):
        diag_x.go_on(j)
    spread_panels(0)
    add_opposite(2)
    diag_x.finish()

    low = lax.broadcasted_iota(jnp.int32, (grid_rows, 32, 128), 2) < 64
    for pair in range(grid_cols // 2):
        left, right = grid_diag[2 * pair], grid_diag[2 * pair + 1]
        lanes = slice(pair * 128, (pair + 1) * 128)
        full_diag[:, 0, :, lanes] = jnp.where(low, left, pltpu.roll(right, 64, 2))
        full_diag[:, 1, :, lanes] = jnp.where(low, pltpu.roll(left, 64, 2), right)
    chosen = (lax.broadcasted_iota(jnp.int32, (width, width), 0) == pivot_ref[...]).astype(BF16)
    full = full_diag[...].reshape(width, width)
    parts = [contract(chosen, x, 0, 0) for x in split3(full)]
    a_ref[...] = parts[0] + parts[1] + parts[2]

    slots = {
        (0, 0): [(finish_sum, 1)],
        (0, 1): [(rows_on, 1), (columns_on, 0)],
        (1, 1): [(columns_on, 1)],
        (1, 2): [(finish_sum, 2)],
        (1, 3): [(rows_on, 2)],
        (2, 3): [(rows_on, 3)],
        (3, 2): [(pass_on, 1)],
    }
    slots = {at: [
            (f, s) for f, s in work if not (f is rows_on and s >= far) and not (f is columns_on and s >= panel_x.steps)
        ]
        for at, work in slots.items()}

    def hook(i, at):
        for (block, place), work in slots.items():
            if place == at and block < blocks and work:
                @pl.when(i == block)
                def _(work=work):
                    for f, s in work:
                        f(s)

    def hooks_after(least, most):
        for (block, place), work in sorted(slots.items()):
            if least <= block <= most:
                for f, s in work:
                    f(s)

    @pl.loop(0, blocks)
    def _(i):
        eliminate_block(a_ref, d_ref, up_ref, i, hook)

    hooks_after(blocks, 4)

    strip = a_ref[pl.ds(pl.multiple_of(c * 64, 64), 64), pl.ds(pl.multiple_of((r // 2) * 128, 128), 128)]
    diagonal = up_ref[c // 2, pl.ds(pl.multiple_of(lax.rem(c, 2) * 64, 64), 64), :]
    strip = jnp.where(r // 2 > c // 2, strip, jnp.where(r // 2 == c // 2, diagonal, 0.0))
    odd = lax.rem(r, 2) == 1
    factor_out[...] = jnp.transpose(jnp.where(odd, pltpu.roll(strip, 64, 1), strip))[:64, :]

    inverse = jnp.where(
        lax.broadcasted_iota(jnp.int32, (width, width), 1) // 128
        <= lax.broadcasted_iota(jnp.int32, (width, width), 0) // 128,
        a_ref[...],
        0.0,
    )
    inv = split2(inverse)
    panel_x.finish()
    tile = 256

    def panel_tile(target, source, factor):
        @pl.loop(0, span // tile)
        def _(t):
            lanes = pl.ds(pl.multiple_of(t * tile, tile), tile)
            target[:, lanes] = dot3(factor, split2(source[:, :, lanes].reshape(width, tile)))

    panel_tile(left_x, all_columns, inv)
    lower_out[...] = left_x[pl.ds(pl.multiple_of(c * 64, 64), 64), :]
    parts = [contract(x, chosen, 1, 1) for x in split3(inverse)]
    inv_pivot = split2(parts[0] + parts[1] + parts[2])
    for d in range(2):
        panel_z(far - 1, d).wait_recv()
    panel_tile(right_x, all_rows, inv_pivot)
    upper_out[...] = right_x[pl.ds(pl.multiple_of(r * 64, 64), 64), :]

    pass_on(2)

    right = split2(right_x[...])

    @pl.loop(0, span // BS)
    def _(t):
        rows = pl.ds(pl.multiple_of(t * BS, BS), BS)
        update[t, :, :] = dot3(split2(jnp.transpose(left_x[:, rows])), right)

    def sent(steps, pieces):
        for s in pieces:
            for t in steps:
                for d in range(2):
                    ring(t, d, s).wait_send()

    sent((1, 2, 3), range(len(SUBS)))
    sent((4, 5, 6), range(1))
    for k in range(1, LAYERS):
        diag_y(k).wait_send()
    for i in range(len(stages)):
        stage_z(i, "send")
    diag_x.drain()
    panel_x.drain()
    for j in range(far):
        for d in range(2):
            panel_z(j, d).wait_send()

    def subtract(k, h, s):
        first, count = SUBS[s]
        into = pl.ds(first - PANEL, count)
        update[k * 2 + h, into, :] = fin[k, h, pl.ds(first, count), :] - update[k * 2 + h, into, :]

    for s in range(1, len(SUBS)):
        for h in range(2):
            subtract(m, h, s)
    for s in range(1, len(SUBS)):
        for d in range(2):
            ring(5, d, s).wait_recv()
        for k in (1, -1):
            for h in range(2):
                subtract(layer(k), h, s)
    sent((4, 5), range(1, len(SUBS)))
    for s in range(1, len(SUBS)):
        for d in range(2):
            ring(6, d, s).wait_recv()
        for h in range(2):
            subtract(layer(2), h, s)
    sent((6,), range(1, len(SUBS)))


def store_kernel(*refs):
    ins, outs, sem = refs[:4], refs[4:8], refs[8]
    copies = [pltpu.make_async_copy(ins[3].at[i], outs[3].at[i], sem.at[3 + i]) for i in range(ins[3].shape[0])]
    copies += [pltpu.make_async_copy(ins[i], outs[i], sem.at[i]) for i in range(3)]
    for copy in copies:
        copy.start()
    for copy in copies:
        copy.wait()


def per_device(diag_parts, column_parts, row_parts, schur_parts, block_pattern, pivot_order):
    rows_dev, cols_dev = schur_parts.shape[1:]
    width = pivot_order.shape[0]
    grid_rows, grid_cols = lax.axis_size("row"), lax.axis_size("col")
    vmem = pl.BlockSpec(memory_space=pltpu.VMEM)
    anywhere = pl.BlockSpec(memory_space=pl.ANY)
    dma = pltpu.SemaphoreType.DMA
    subs = len(SUBS)
    chips = max(grid_cols // 4, 1)
    shapes = (
        diag_parts.shape[1:],
        column_parts.shape[:0:-1],
        row_parts.shape[1:],
        (rows_dev // BS, BS, cols_dev),
    )
    held = pl.pallas_call(
        functools.partial(kernel, grid_rows, grid_cols),
        out_shape=tuple(pltpu.VMEM(shape, F32) for shape in shapes),
        in_specs=[pl.BlockSpec(memory_space=pltpu.HBM)] * 6,
        out_specs=[vmem] * 4,
        scratch_shapes=[
            pltpu.VMEM(diag_parts.shape[1:], F32),
            pltpu.VMEM(block_pattern.shape[1:], jnp.int32),
            pltpu.VMEM((1, width), jnp.int32),
            pltpu.VMEM((LAYERS, 2, HALF, cols_dev), F32),
            pltpu.VMEM((LAYERS, 2, HALF, cols_dev), F32),
            pltpu.VMEM((2, HALF, cols_dev), F32),
            pltpu.VMEM((2, 2, HALF, cols_dev), F32),
            pltpu.VMEM((rows_dev // BS, cols_dev), F32),
            pltpu.VMEM((LAYERS, 32, 128), F32),
            pltpu.VMEM((grid_cols, grid_rows, 32, 128), F32),
            pltpu.VMEM((grid_rows, 2, 32, width), F32),
            pltpu.VMEM((grid_cols, 64, rows_dev), F32),
            pltpu.VMEM((grid_rows, 64, cols_dev), F32),
            pltpu.VMEM((width, width), F32),
            pltpu.VMEM((128, 128), F32),
            pltpu.VMEM((width // 128, 128, 128), F32),
            pltpu.VMEM((width, rows_dev), F32),
            pltpu.VMEM((width, cols_dev), F32),
            dma((19,)),
            dma((6, 2, subs)),
            dma((6, 2, subs)),
            dma((LAYERS - 1,)),
            dma((LAYERS - 1,)),
            dma((grid_rows - 1, 2)),
            dma((grid_rows - 1, 2)),
            dma((chips, 2)),
            dma((chips, 2)),
            dma((1 + 2 * chips,)),
            dma((1 + 2 * chips,)),
            dma((grid_rows // 2, 2)),
            dma((grid_rows // 2, 2)),
            dma((chips, 2)),
            dma((chips, 2)),
            dma((1 + 2 * chips,)),
            dma((1 + 2 * chips,)),
            pltpu.SemaphoreType.REGULAR((2, 2)),
            pltpu.SemaphoreType.REGULAR((4,)),
            pltpu.SemaphoreType.REGULAR,
        ],
        compiler_params=pltpu.CompilerParams(
            collective_id=0, has_side_effects=True, vmem_limit_bytes=48 << 20
        ),
    )(
        *(
            pltpu.with_memory_space_constraint(x, pltpu.HBM)
            for x in (
                diag_parts[0],
                block_pattern[0],
                pivot_order.reshape(1, width),
                column_parts[0].T,
                row_parts[0],
                schur_parts[0],
            )
        )
    )
    factor, lower_t, upper, schur = pl.pallas_call(
        store_kernel,
        out_shape=tuple(jax.ShapeDtypeStruct(shape, F32) for shape in shapes),
        in_specs=[vmem] * 4,
        out_specs=[anywhere] * 4,
        scratch_shapes=[dma((3 + rows_dev // BS,))],
        compiler_params=pltpu.CompilerParams(vmem_limit_bytes=8 << 20),
    )(*held)
    return factor, lower_t.T, upper, schur.reshape(rows_dev, cols_dev)


def solution(mesh):
    placed = (
        P("gz", "row", "col"),
        P("gz", "row", "col"),
        P("gz", "row", "col"),
        P("gz", "row", "col"),
        P("gz", "row", "col"),
        P(),
    )
    return jax.shard_map(
        per_device,
        mesh=mesh,
        in_specs=placed,
        out_specs=(P("row", "col"), P("row", "col"), P("row", "col"), P("row", "col")),
        check_vma=False,
    )
```

```python
import functools

import jax
import jax.numpy as jnp
from jax import lax
from jax.experimental import pallas as pl
from jax.experimental.pallas import tpu as pltpu
from jax.sharding import PartitionSpec as P

BS = 128
LAYERS = 4
PANEL = 16
HALF = PANEL + BS
SUBS = ((0, 16), (16, 64), (80, 64))
HI = lax.Precision.HIGHEST
F32 = jnp.float32
BF16 = jnp.bfloat16
MESH = pl.DeviceIdType.MESH


def split2(x):
    hi = x.astype(BF16)
    return hi, (x - hi.astype(F32)).astype(BF16)


def split3(x):
    hi = x.astype(BF16)
    rest = x - hi.astype(F32)
    mid = rest.astype(BF16)
    return hi, mid, (rest - mid.astype(F32)).astype(BF16)


def contract(a, b, da, db):
    return lax.dot_general(a, b, (((da,), (db,)), ((), ())), preferred_element_type=F32)


def dot3(a, b):
    return contract(a[0], b[0], 1, 0) + (contract(a[0], b[1], 1, 0) + contract(a[1], b[0], 1, 0))


def eliminate_group(d_ref, q):
    lane = lax.broadcasted_iota(jnp.int32, (8, 128), 1)
    sub = lax.broadcasted_iota(jnp.int32, (8, 128), 0)
    lo = 8 * q
    g = d_ref[lo : lo + 8, :]
    col = [jnp.broadcast_to(g[:, lo + j : lo + j + 1], (8, 128)) for j in range(8)]
    snap = jnp.zeros((8, 128), F32)
    pivots = jnp.ones((8, 128), F32)
    for k in range(8):
        piv = jnp.broadcast_to(col[k][k : k + 1, :], (8, 128))
        f = jnp.where(sub != k, col[k] * (1.0 / piv), 0.0)
        for j in range(k + 1, 8):
            col[j] = col[j] - f * jnp.broadcast_to(col[j][k : k + 1, :], (8, 128))
        g = jnp.where(lane == lo + k, jnp.where(sub == k, 1.0, 0.0), g)
        top = jnp.broadcast_to(g[k : k + 1, :], (8, 128))
        snap = jnp.where(sub == k, top, snap)
        pivots = jnp.where(sub == k, piv, pivots)
        g = g - f * top
    w = g / pivots
    if q < 15:
        below = d_ref[lo + 8 : lo + 16, :]
        acc = jnp.where((lane >= lo) & (lane < lo + 8), 0.0, below)
        for j in range(8):
            acc = acc - jnp.broadcast_to(below[:, lo + j : lo + j + 1], (8, 128)) * jnp.broadcast_to(
                w[j : j + 1, :], (8, 128)
            )
        d_ref[lo + 8 : lo + 16, :] = acc
    if q < 14:
        gh, gm, gl = (x.astype(F32) for x in split3(d_ref[lo : lo + 8, :]))
        wh, wm, wl = (x.astype(F32) for x in split3(w))
        update = contract(
            jnp.concatenate([gh, gh, gm, gh, gm, gl], axis=0).astype(BF16),
            jnp.concatenate([wh, wm, wh, wl, wm, wh], axis=0).astype(BF16),
            0,
            0,
        )
        rest = d_ref[lo + 16 : 128, :]
        lane_r = lax.broadcasted_iota(jnp.int32, rest.shape, 1)
        d_ref[lo + 16 : 128, :] = jnp.where((lane_r >= lo) & (lane_r < lo + 8), 0.0, rest) - update[lo + 16 :, :]
    d_ref[lo : lo + 8, :] = jnp.where(lane == lo + sub, 1.0, snap) * lax.rsqrt(pivots)
    return jnp.sqrt(pivots)


def eliminate_block(a_ref, d_ref, up_ref, i, hook):
    width = a_ref.shape[0]
    at = pl.multiple_of(i * 128, 128)
    rows = pl.ds(at, 128)
    d_ref[...] = a_ref[rows, pl.ds(at, 128)]
    diagonal = []
    for q in range(16):
        if q % 4 == 0:
            hook(i, q // 4)
        diagonal.append(eliminate_group(d_ref, q))
    r = lax.broadcasted_iota(jnp.int32, (128, 128), 0)
    c = lax.broadcasted_iota(jnp.int32, (128, 128), 1)
    d = d_ref[...]
    inverse = jnp.where(c <= r, d, 0.0)
    upper = jnp.where(c > r, d, jnp.where(c == r, jnp.concatenate(diagonal, axis=0), 0.0))
    up_ref[i] = upper
    a_ref[rows, :] = jnp.dot(inverse, a_ref[rows, :], precision=HI, preferred_element_type=F32)
    a_ref[rows, pl.ds(at, 128)] = inverse

    @pl.loop(i + 1, width // 128)
    def _(j):
        below = pl.ds(pl.multiple_of(j * 128, 128), 128)
        a_ref[below, pl.ds(at, 128)] = jnp.zeros((128, 128), F32)
        a_ref[below, :] = a_ref[below, :] - lax.dot_general(
            a_ref[rows, below], a_ref[rows, :], (((0,), (0,)), ((), ())), precision=HI, preferred_element_type=F32
        )


def kernel(
    grid_rows, grid_cols,
    diag_hbm, pattern_hbm, pivot_hbm, column_ref, row_ref, schur_ref,
    factor_out, lower_out, upper_out, update,
    diag_ref, pattern_ref, pivot_ref, w, fin, rs1, rsx, weights,
    layer_diag, grid_diag, full_diag, all_columns, all_rows, a_ref, d_ref, up_ref, left_x, right_x,
    load_sem, y_send, y_recv, dy_send, dy_recv, dz_send, dz_recv, dx_send, dx_recv, dc_send, dc_recv,
    pz_send, pz_recv, px_send, px_recv, pc_send, pc_recv, x_word, beside_in, all_in,
):
    m = lax.axis_index("gz")
    r = lax.axis_index("row")
    c = lax.axis_index("col")
    width = a_ref.shape[0]
    span = fin.shape[3]
    blocks = width // 128

    def layer(k):
        return lax.rem(m + k + LAYERS, LAYERS)

    def row_peer(k):
        return lax.rem(r + k + grid_rows, grid_rows)

    def col_peer(k):
        return lax.rem(c + k + grid_cols, grid_cols)

    other_core = c + 1 - 2 * lax.rem(c, 2)

    def in_line(here, step, count):
        return jnp.logical_and(here + step >= 0, here + step < count)

    barrier = pltpu.get_barrier_semaphore()
    for k in (1, 3, 2):
        pl.semaphore_signal(barrier, inc=1, device_id=(layer(k), r, c), device_id_type=MESH)
    sides = [(r, 1, grid_rows), (r, -1, grid_rows), (c, 2, grid_cols), (c, -2, grid_cols)]

    def side(i):
        step = sides[i][1]
        place = (m, row_peer(step), c) if i < 2 else (m, r, col_peer(step))
        return place, in_line(*sides[i])

    for i in range(4):
        place, there = side(i)

        @pl.when(jnp.logical_and(there, m == 0))
        def _(place=place):
            pl.semaphore_signal(barrier, inc=1, device_id=place, device_id_type=MESH)

    pl.semaphore_signal(barrier, inc=1, device_id=(m, r, other_core), device_id_type=MESH)

    small = [
        pltpu.make_async_copy(x, y, load_sem.at[16 + i])
        for i, (x, y) in enumerate(((diag_hbm, diag_ref), (pattern_hbm, pattern_ref), (pivot_hbm, pivot_ref)))
    ]

    def load_panel(k, h):
        block = k * 2 + h
        return pltpu.make_async_copy(
            (column_ref, row_ref)[h].at[pl.ds(pl.multiple_of(k * PANEL, PANEL), PANEL), :],
            w.at[k, h, pl.ds(0, PANEL), :],
            load_sem.at[8 + block],
        )

    def load_front(k, h):
        block = k * 2 + h
        return pltpu.make_async_copy(
            schur_ref.at[pl.ds(pl.multiple_of(block * BS, BS), BS), :],
            w.at[k, h, pl.ds(PANEL, BS), :],
            load_sem.at[block],
        )

    order = [(layer(k), h) for k in (2, 1, -1, 0) for h in range(2)]
    small[0].start()
    for k, h in order:
        load_panel(k, h).start()
    for load in small[1:]:
        load.start()
    for k, h in order:
        load_front(k, h).start()

    def ring(t, d, s):
        step = 1 - 2 * d
        to = layer(step)
        first, count = SUBS[s]
        rows = pl.ds(first, count)
        if t == 1:
            src, dst = w.at[layer(2), d, rows], rs1.at[d, rows]
        elif t == 2:
            src, dst = w.at[to, 1 - d, rows], rsx.at[d, 1 - d, rows]
        elif t == 3:
            src, dst = w.at[to, d, rows], rsx.at[d, d, rows]
        elif t == 4:
            src = dst = fin.at[m, d, rows]
        elif t == 5:
            src = dst = fin.at[m, 1 - d, rows]
        else:
            src = dst = fin.at[layer(-step), d, rows]
        return pltpu.make_async_remote_copy(
            src_ref=src, dst_ref=dst, send_sem=y_send.at[t - 1, d, s], recv_sem=y_recv.at[t - 1, d, s],
            device_id=(to, r, c), device_id_type=MESH,
        )

    def add_opposite(s):
        first, count = SUBS[s]
        rows = pl.ds(first, count)
        for d in range(2):
            ring(1, d, s).wait_recv()
            to = layer(1 - 2 * d)
            w[to, d, rows, :] = w[to, d, rows, :] + rs1[d, rows, :]
            ring(3, d, s).start()

    def finish_sum(s):
        first, count = SUBS[s]
        rows = pl.ds(first, count)
        for d in range(2):
            ring(2, d, s).wait_recv()
            ring(3, d, s).wait_recv()
        for h in range(2):
            fin[m, h, rows, :] = w[m, h, rows, :] + rsx[0, h, rows, :] + rsx[1, h, rows, :]
        for t in (4, 5):
            for d in range(2):
                ring(t, d, s).start()

    def pass_on(s):
        for d in range(2):
            ring(4, d, s).wait_recv()
            ring(6, d, s).start()

    def arrived(s):
        for d in range(2):
            ring(5, d, s).wait_recv()
            ring(6, d, s).wait_recv()

    def diag_y(k):
        return pltpu.make_async_remote_copy(
            src_ref=layer_diag.at[m], dst_ref=layer_diag.at[m], send_sem=dy_send.at[k - 1], recv_sem=dy_recv.at[k - 1],
            device_id=(layer(k), r, c), device_id_type=MESH,
        )

    stages = [[k for k in stage if k < grid_rows] for stage in ((1,), (2,), (3, 4), (5, 6, 7))]

    def along_z(k, act):
        for d in range(2):
            to = r + k * (1 - 2 * d)
            copy = pltpu.make_async_remote_copy(
                src_ref=grid_diag.at[c, r], dst_ref=grid_diag.at[c, r],
                send_sem=dz_send.at[k - 1, d], recv_sem=dz_recv.at[k - 1, d],
                device_id=(m, lax.rem(to + grid_rows, grid_rows), c), device_id_type=MESH,
            )
            ahead, behind = to < grid_rows, to >= 0
            if act == "recv":
                ahead, behind = r - k * (1 - 2 * d) < grid_rows, r - k * (1 - 2 * d) >= 0

            @pl.when(jnp.logical_and(ahead, behind))
            def _(copy=copy):
                if act == "start":
                    copy.start()
                elif act == "recv":
                    copy.wait_recv()
                else:
                    copy.wait_send()

    def stage_z(i, act):
        for k in stages[i]:
            along_z(k, act)

    class AlongX:
        def __init__(self, ref, sems):
            self.ref, self.sems, self.steps = ref, sems, grid_cols // 4

        def part(self, j, d):
            block = col_peer(2 * j * (2 * d - 1))
            if j == self.steps - 1:
                half = self.ref.shape[1] // 2
                return self.ref.at[block, pl.ds(half * d, half)]
            return self.ref.at[block]

        def chip(self, j, d):
            ref = self.part(j, d)
            return pltpu.make_async_remote_copy(
                src_ref=ref, dst_ref=ref, send_sem=self.sems[0].at[j, d], recv_sem=self.sems[1].at[j, d],
                device_id=(m, r, col_peer(2 - 4 * d)), device_id_type=MESH,
            )

        def core(self, i):
            if i == 0:
                ref = self.ref.at[c]
            else:
                j, d = divmod(i - 1, 2)
                block = col_peer(2 * (j + 1) * (2 * d - 1))
                ref = self.ref.at[block]
                if j == self.steps - 1:
                    half = self.ref.shape[1] // 2
                    ref = self.ref.at[block, pl.ds(half * d, half)]
            return pltpu.make_async_remote_copy(
                src_ref=ref, dst_ref=ref, send_sem=self.sems[2].at[i], recv_sem=self.sems[3].at[i],
                device_id=(m, r, other_core), device_id_type=MESH,
            )

        def start(self):
            for d in range(2):
                if self.steps:
                    self.chip(0, d).start()
            self.core(0).start()

        def go_on(self, j):
            for d in range(2):
                self.chip(j, d).wait_recv()
                if j + 1 < self.steps:
                    self.chip(j + 1, d).start()
                self.core(1 + 2 * j + d).start()

        def finish(self):
            for i in range(1 + 2 * self.steps):
                self.core(i).wait_recv()

        def drain(self):
            for i in range(1 + 2 * self.steps):
                self.core(i).wait_send()
            for j in range(self.steps):
                for d in range(2):
                    self.chip(j, d).wait_send()

    diag_x = AlongX(grid_diag, (dx_send, dx_recv, dc_send, dc_recv))
    panel_x = AlongX(all_columns, (px_send, px_recv, pc_send, pc_recv))

    def send(t, s):
        for d in range(2):
            ring(t, d, s).start()

    def mask_front(k, h):
        load_front(k, h).wait()
        w[k, h, PANEL:HALF, :] = w[k, h, PANEL:HALF, :] * weights[pl.ds(k * 2 + h, 1), :]

    words = max(grid_cols // 2 - 2, 0)

    def word(i, act):
        for d in range(2):
            step = 2 - 4 * d
            @pl.when(in_line(c, step if act == "send" else -step, grid_cols))
            def _(d=d, step=step):
                if act == "send":
                    pl.semaphore_signal(
                        x_word.at[i, d], inc=1, device_id=(m, r, col_peer(step)), device_id_type=MESH
                    )
                else:
                    pl.semaphore_wait(x_word.at[i, d], 1)

    small[0].wait()
    layer_diag[m] = jnp.concatenate([diag_ref[:32, :], diag_ref[32:, :]], axis=1)
    beside = sum(in_line(*at).astype(jnp.int32) for at in sides)
    pl.semaphore_wait(barrier, LAYERS - 1 + 1 + jnp.where(m == 0, beside, 0))

    def layers_in():
        for i in range(4):
            place, there = side(i)

            @pl.when(jnp.logical_and(there, m == 0))
            def _(i=i, place=place):
                pl.semaphore_signal(beside_in.at[i ^ 1], inc=1, device_id=place, device_id_type=MESH)

    def sides_in():
        for i in range(4):
            _, there = side(i)

            @pl.when(jnp.logical_and(there, m == 0))
            def _(i=i):
                pl.semaphore_wait(beside_in.at[i], 1)

        @pl.when(m == 0)
        def _():
            for k in range(1, LAYERS):
                pl.semaphore_signal(all_in, inc=1, device_id=(layer(k), r, c), device_id_type=MESH)

        @pl.when(m != 0)
        def _():
            pl.semaphore_wait(all_in, 1)

    layers_in()
    for k in range(1, LAYERS):
        diag_y(k).start()
    for k, h in order[:6]:
        load_panel(k, h).wait()
    send(1, 0)
    send(2, 0)
    for load in small[1:]:
        load.wait()
    pattern = pattern_ref[...].astype(F32)
    weights[...] = jnp.concatenate(
        [jnp.broadcast_to(pattern[:, j : j + 1], (pattern.shape[0], BS)) for j in range(pattern.shape[1])], axis=1
    )
    for k, h in order[:2]:
        mask_front(k, h)
    send(1, 1)
    for k in range(1, LAYERS):
        diag_y(k).wait_recv()
    grid_diag[c, r] = layer_diag[0] + layer_diag[1] + layer_diag[2] + layer_diag[3]
    sides_in()
    stage_z(0, "start")
    if words:
        word(0, "send")
    add_opposite(0)
    send(1, 2)
    for i in range(words):
        word(i, "wait")
        if i + 1 < words:
            word(i + 1, "send")
    for k, h in order[2:6]:
        mask_front(k, h)
    stage_z(0, "recv")
    stage_z(1, "start")
    for k, h in order[6:]:
        load_panel(k, h).wait()
        mask_front(k, h)
    stage_z(1, "recv")
    stage_z(2, "start")
    finish_sum(0)
    send(2, 1)
    stage_z(2, "recv")
    stage_z(3, "start")
    pass_on(0)
    send(2, 2)
    stage_z(3, "recv")
    diag_x.start()

    far = grid_rows // 2

    def panel_z(j, d):
        step = 1 - 2 * d
        block = row_peer(-step * j)
        ref = all_rows.at[block, pl.ds(32 * d, 32)] if j == far - 1 else all_rows.at[block]
        return pltpu.make_async_remote_copy(
            src_ref=ref, dst_ref=ref, send_sem=pz_send.at[j, d], recv_sem=pz_recv.at[j, d],
            device_id=(m, row_peer(step), c), device_id_type=MESH,
        )

    def spread_panels(s):
        arrived(s)
        for k in range(LAYERS):
            all_columns[c, k * PANEL : (k + 1) * PANEL, :] = fin[k, 0, 0:PANEL, :]
            all_rows[r, k * PANEL : (k + 1) * PANEL, :] = fin[k, 1, 0:PANEL, :]
        for d in range(2):
            panel_z(0, d).start()
        panel_x.start()

    def rows_on(j):
        for d in range(2):
            panel_z(j - 1, d).wait_recv()
            panel_z(j, d).start()

    def columns_on(j):
        panel_x.go_on(j)

    add_opposite(1)
    for j in range(diag_x.steps):
        diag_x.go_on(j)
    spread_panels(0)
    add_opposite(2)
    diag_x.finish()

    low = lax.broadcasted_iota(jnp.int32, (grid_rows, 32, 128), 2) < 64
    for pair in range(grid_cols // 2):
        left, right = grid_diag[2 * pair], grid_diag[2 * pair + 1]
        lanes = slice(pair * 128, (pair + 1) * 128)
        full_diag[:, 0, :, lanes] = jnp.where(low, left, pltpu.roll(right, 64, 2))
        full_diag[:, 1, :, lanes] = jnp.where(low, pltpu.roll(left, 64, 2), right)
    chosen = (lax.broadcasted_iota(jnp.int32, (width, width), 0) == pivot_ref[...]).astype(BF16)
    full = full_diag[...].reshape(width, width)
    parts = [contract(chosen, x, 0, 0) for x in split3(full)]
    a_ref[...] = parts[0] + parts[1] + parts[2]

    slots = {
        (0, 0): [(finish_sum, 1)],
        (0, 1): [(rows_on, 1), (columns_on, 0)],
        (1, 1): [(columns_on, 1)],
        (1, 2): [(finish_sum, 2)],
        (1, 3): [(rows_on, 2)],
        (2, 3): [(rows_on, 3)],
        (3, 2): [(pass_on, 1)],
    }
    slots = {at: [
            (f, s) for f, s in work if not (f is rows_on and s >= far) and not (f is columns_on and s >= panel_x.steps)
        ]
        for at, work in slots.items()}

    def hook(i, at):
        for (block, place), work in slots.items():
            if place == at and block < blocks and work:
                @pl.when(i == block)
                def _(work=work):
                    for f, s in work:
                        f(s)

    def hooks_after(least, most):
        for (block, place), work in sorted(slots.items()):
            if least <= block <= most:
                for f, s in work:
                    f(s)

    @pl.loop(0, blocks)
    def _(i):
        eliminate_block(a_ref, d_ref, up_ref, i, hook)

    hooks_after(blocks, 4)

    strip = a_ref[pl.ds(pl.multiple_of(c * 64, 64), 64), pl.ds(pl.multiple_of((r // 2) * 128, 128), 128)]
    diagonal = up_ref[c // 2, pl.ds(pl.multiple_of(lax.rem(c, 2) * 64, 64), 64), :]
    strip = jnp.where(r // 2 > c // 2, strip, jnp.where(r // 2 == c // 2, diagonal, 0.0))
    odd = lax.rem(r, 2) == 1
    factor_out[...] = jnp.transpose(jnp.where(odd, pltpu.roll(strip, 64, 1), strip))[:64, :]

    inverse = jnp.where(
        lax.broadcasted_iota(jnp.int32, (width, width), 1) // 128
        <= lax.broadcasted_iota(jnp.int32, (width, width), 0) // 128,
        a_ref[...],
        0.0,
    )
    inv = split2(inverse)
    panel_x.finish()
    tile = 256

    def panel_tile(target, source, factor):
        @pl.loop(0, span // tile)
        def _(t):
            lanes = pl.ds(pl.multiple_of(t * tile, tile), tile)
            target[:, lanes] = dot3(factor, split2(source[:, :, lanes].reshape(width, tile)))

    panel_tile(left_x, all_columns, inv)
    lower_out[...] = left_x[pl.ds(pl.multiple_of(c * 64, 64), 64), :]
    parts = [contract(x, chosen, 1, 1) for x in split3(inverse)]
    inv_pivot = split2(parts[0] + parts[1] + parts[2])
    for d in range(2):
        panel_z(far - 1, d).wait_recv()
    panel_tile(right_x, all_rows, inv_pivot)
    upper_out[...] = right_x[pl.ds(pl.multiple_of(r * 64, 64), 64), :]

    pass_on(2)

    right = split2(right_x[...])

    @pl.loop(0, span // BS)
    def _(t):
        rows = pl.ds(pl.multiple_of(t * BS, BS), BS)
        update[t, :, :] = dot3(split2(jnp.transpose(left_x[:, rows])), right)

    def sent(steps, pieces):
        for s in pieces:
            for t in steps:
                for d in range(2):
                    ring(t, d, s).wait_send()

    sent((1, 2, 3), range(len(SUBS)))
    sent((4, 5, 6), range(1))
    for k in range(1, LAYERS):
        diag_y(k).wait_send()
    for i in range(len(stages)):
        stage_z(i, "send")
    diag_x.drain()
    panel_x.drain()
    for j in range(far):
        for d in range(2):
            panel_z(j, d).wait_send()

    def subtract(k, h, s):
        first, count = SUBS[s]
        into = pl.ds(first - PANEL, count)
        update[k * 2 + h, into, :] = fin[k, h, pl.ds(first, count), :] - update[k * 2 + h, into, :]

    for s in range(1, len(SUBS)):
        for h in range(2):
            subtract(m, h, s)
    for s in range(1, len(SUBS)):
        for d in range(2):
            ring(5, d, s).wait_recv()
        for k in (1, -1):
            for h in range(2):
                subtract(layer(k), h, s)
    sent((4, 5), range(1, len(SUBS)))
    for s in range(1, len(SUBS)):
        for d in range(2):
            ring(6, d, s).wait_recv()
        for h in range(2):
            subtract(layer(2), h, s)
    sent((6,), range(1, len(SUBS)))


def store_kernel(*refs):
    ins, outs, sem = refs[:4], refs[4:8], refs[8]
    copies = [pltpu.make_async_copy(ins[i], outs[i], sem.at[i]) for i in (3, 0, 1, 2)]
    for copy in copies:
        copy.start()
    for copy in copies:
        copy.wait()


def per_device(diag_parts, column_parts, row_parts, schur_parts, block_pattern, pivot_order):
    rows_dev, cols_dev = schur_parts.shape[1:]
    width = pivot_order.shape[0]
    grid_rows, grid_cols = lax.axis_size("row"), lax.axis_size("col")
    vmem = pl.BlockSpec(memory_space=pltpu.VMEM)
    anywhere = pl.BlockSpec(memory_space=pl.ANY)
    dma = pltpu.SemaphoreType.DMA
    subs = len(SUBS)
    chips = max(grid_cols // 4, 1)
    shapes = (
        diag_parts.shape[1:],
        column_parts.shape[:0:-1],
        row_parts.shape[1:],
        (rows_dev // BS, BS, cols_dev),
    )
    held = pl.pallas_call(
        functools.partial(kernel, grid_rows, grid_cols),
        out_shape=tuple(pltpu.VMEM(shape, F32) for shape in shapes),
        in_specs=[pl.BlockSpec(memory_space=pltpu.HBM)] * 6,
        out_specs=[vmem] * 4,
        scratch_shapes=[
            pltpu.VMEM(diag_parts.shape[1:], F32),
            pltpu.VMEM(block_pattern.shape[1:], jnp.int32),
            pltpu.VMEM((1, width), jnp.int32),
            pltpu.VMEM((LAYERS, 2, HALF, cols_dev), F32),
            pltpu.VMEM((LAYERS, 2, HALF, cols_dev), F32),
            pltpu.VMEM((2, HALF, cols_dev), F32),
            pltpu.VMEM((2, 2, HALF, cols_dev), F32),
            pltpu.VMEM((rows_dev // BS, cols_dev), F32),
            pltpu.VMEM((LAYERS, 32, 128), F32),
            pltpu.VMEM((grid_cols, grid_rows, 32, 128), F32),
            pltpu.VMEM((grid_rows, 2, 32, width), F32),
            pltpu.VMEM((grid_cols, 64, rows_dev), F32),
            pltpu.VMEM((grid_rows, 64, cols_dev), F32),
            pltpu.VMEM((width, width), F32),
            pltpu.VMEM((128, 128), F32),
            pltpu.VMEM((width // 128, 128, 128), F32),
            pltpu.VMEM((width, rows_dev), F32),
            pltpu.VMEM((width, cols_dev), F32),
            dma((19,)),
            dma((6, 2, subs)),
            dma((6, 2, subs)),
            dma((LAYERS - 1,)),
            dma((LAYERS - 1,)),
            dma((grid_rows - 1, 2)),
            dma((grid_rows - 1, 2)),
            dma((chips, 2)),
            dma((chips, 2)),
            dma((1 + 2 * chips,)),
            dma((1 + 2 * chips,)),
            dma((grid_rows // 2, 2)),
            dma((grid_rows // 2, 2)),
            dma((chips, 2)),
            dma((chips, 2)),
            dma((1 + 2 * chips,)),
            dma((1 + 2 * chips,)),
            pltpu.SemaphoreType.REGULAR((2, 2)),
            pltpu.SemaphoreType.REGULAR((4,)),
            pltpu.SemaphoreType.REGULAR,
        ],
        compiler_params=pltpu.CompilerParams(
            collective_id=0, has_side_effects=True, vmem_limit_bytes=48 << 20
        ),
    )(
        *(
            pltpu.with_memory_space_constraint(x, pltpu.HBM)
            for x in (
                diag_parts[0],
                block_pattern[0],
                pivot_order.reshape(1, width),
                column_parts[0].T,
                row_parts[0],
                schur_parts[0],
            )
        )
    )
    factor, lower_t, upper, schur = pl.pallas_call(
        store_kernel,
        out_shape=tuple(jax.ShapeDtypeStruct(shape, F32) for shape in shapes),
        in_specs=[vmem] * 4,
        out_specs=[anywhere] * 4,
        scratch_shapes=[dma((4,))],
        compiler_params=pltpu.CompilerParams(vmem_limit_bytes=8 << 20),
    )(*held)
    return factor, lower_t.T, upper, schur.reshape(rows_dev, cols_dev)


def solution(mesh):
    placed = (
        P("gz", "row", "col"),
        P("gz", "row", "col"),
        P("gz", "row", "col"),
        P("gz", "row", "col"),
        P("gz", "row", "col"),
        P(),
    )
    return jax.shard_map(
        per_device,
        mesh=mesh,
        in_specs=placed,
        out_specs=(P("row", "col"), P("row", "col"), P("row", "col"), P("row", "col")),
        check_vma=False,
    )
```
